32 devices in a mesh: mod: 2 (over x), dp: 16 (over z, y, core).
Axes of the slice: x: 2, y: 2, z: 4, core: 2. Of those that a mesh axis runs over, the one named last changes fastest.
Arguments:
- text: bfloat16 [128, 40, 768], P(('mod', 'dp')), may hold values from -6 to 6
- lengths: int32 [128], P(('mod', 'dp')), may hold values from 8 to 40, as said below
- patches: bfloat16 [128, 145, 1024], P(('mod', 'dp')), may hold values from -6 to 6
- w_query: bfloat16 [768, 768], P(('mod', 'dp')), may hold values from -0.21875 to 0.21875
- w_key: bfloat16 [768, 768], P(('mod', 'dp')), may hold values from -0.21875 to 0.21875
- w_value: bfloat16 [768, 768], P(('mod', 'dp')), may hold values from -0.21875 to 0.21875
- w_out: bfloat16 [768, 768], P(('mod', 'dp')), may hold values from -0.625 to 0.625
- b_query: float32 [768], replicated, may hold values from -3 to 3
- b_value: float32 [768], replicated, may hold values from -3 to 3
- b_out: float32 [768], replicated, may hold values from -3 to 3
- gain_one: float32 [768], replicated, may hold values from 0.5 to 1.5
- bias_one: float32 [768], replicated, may hold values from -3 to 3
- w_image: bfloat16 [1024, 768], P(('mod', 'dp')), may hold values from -0.1875 to 0.1875
- b_image: float32 [768], replicated, may hold values from -3 to 3
- c_query: bfloat16 [768, 768], P(('mod', 'dp')), may hold values from -0.21875 to 0.21875
- c_key: bfloat16 [768, 768], P(('mod', 'dp')), may hold values from -0.21875 to 0.21875
- c_value: bfloat16 [768, 768], P(('mod', 'dp')), may hold values from -0.21875 to 0.21875
- c_out: bfloat16 [768, 768], P(('mod', 'dp')), may hold values from -0.875 to 0.875
- cb_query: float32 [768], replicated, may hold values from -3 to 3
- cb_value: float32 [768], replicated, may hold values from -3 to 3
- cb_out: float32 [768], replicated, may hold values from -3 to 3
- gain_two: float32 [768], replicated, may hold values from 0.5 to 1.5
- bias_two: float32 [768], replicated, may hold values from -3 to 3
- w_inner: bfloat16 [768, 3072], P(('mod', 'dp')), may hold values from -0.21875 to 0.21875
- b_inner: float32 [3072], replicated, may hold values from -3 to 3
- w_outer: bfloat16 [3072, 768], P(('mod', 'dp')), may hold values from -0.21875 to 0.21875
- b_outer: float32 [768], replicated, may hold values from -3 to 3
- gain_three: float32 [768], replicated, may hold values from 0.5 to 1.5
- bias_three: float32 [768], replicated, may hold values from -3 to 3
- cotangent: bfloat16 [128, 40, 768], P(('mod', 'dp')), may hold values from -6 to 6
Outputs:
- mixed_out: float32 [128, 40, 768], P(('mod', 'dp'))
- grad_text: float32 [128, 40, 768], P(('mod', 'dp'))
- grad_patches: float32 [128, 145, 1024], P(('mod', 'dp'))
- grad_w_query: float32 [768, 768], P(('mod', 'dp'))
- grad_w_key: float32 [768, 768], P(('mod', 'dp'))
- grad_w_value: float32 [768, 768], P(('mod', 'dp'))
- grad_w_out: float32 [768, 768], P(('mod', 'dp'))
- grad_b_query: float32 [768], replicated
- grad_b_value: float32 [768], replicated
- grad_b_out: float32 [768], replicated
- grad_gain_one: float32 [768], replicated
- grad_bias_one: float32 [768], replicated
- grad_w_image: float32 [1024, 768], P(('mod', 'dp'))
- grad_b_image: float32 [768], replicated
- grad_c_query: float32 [768, 768], P(('mod', 'dp'))
- grad_c_key: float32 [768, 768], P(('mod', 'dp'))
- grad_c_value: float32 [768, 768], P(('mod', 'dp'))
- grad_c_out: float32 [768, 768], P(('mod', 'dp'))
- grad_cb_query: float32 [768], replicated
- grad_cb_value: float32 [768], replicated
- grad_cb_out: float32 [768], replicated
- grad_gain_two: float32 [768], replicated
- grad_bias_two: float32 [768], replicated
- grad_w_inner: float32 [768, 3072], P(('mod', 'dp'))
- grad_b_inner: float32 [3072], replicated
- grad_w_outer: float32 [3072, 768], P(('mod', 'dp'))
- grad_b_outer: float32 [768], replicated
- grad_gain_three: float32 [768], replicated
- grad_bias_three: float32 [768], replicated
The draws below stay inside these ranges and needn't reach their ends.
Inputs may be any that keep to these rules, and one draw needn't show every extreme that they name: `lengths`: real tokens of each item; some item has exactly 40 and some exactly 8.
All inputs are finite; a program needn't handle non-finite values.
Results may differ from the reference program's by a relative error of at most 0.025.
Values may be sent and summed in bfloat16 or wider, within the bound.
No kernel may reach another device: no remote copies, remote signals or barrier semaphores. Data moves between devices by JAX's collectives and lax.ppermute only.
A program may use at most 192 MiB of HBM per device.

```python
import jax
import jax.numpy as jnp
from jax import lax

D = 768
HEADS = 12
HEAD_DIM = 64
FF = 3072
VW = 1024
NP = 145
SEQ = 40
MIN_LEN = 8
ITEMS = 128


def draw_lengths(key, part):
    key = jax.random.fold_in(key, 11)
    key_lengths, key_long, key_offset = jax.random.split(key, 3)
    lengths = jax.random.randint(key_lengths, (ITEMS,), MIN_LEN, SEQ + 1)
    longest = jax.random.randint(key_long, (), 0, ITEMS)
    offset = jax.random.randint(key_offset, (), 1, ITEMS)
    shortest = (longest + offset) % ITEMS
    lengths = lengths.at[longest].set(SEQ)
    lengths = lengths.at[shortest].set(MIN_LEN)
    return lengths.astype(jnp.int32)


def raised(drawn, key, source, target, blocks, factor):
    def block_of(axis_at):
        return (jnp.arange(drawn.shape[axis_at]) // (drawn.shape[axis_at] // blocks)).reshape((-1,) + (1,) * (drawn.ndim - 1 - axis_at))

    near = jax.random.permutation(key, blocks)[block_of(target)]
    second = (block_of(target) + blocks // 2) % blocks
    return jnp.where((block_of(source) == near) | (block_of(source) == second), factor * drawn, drawn)


def levels(own_key, extent, cuts, low, top_value):
    def one(dim, shards_of):
        steps = jax.random.uniform(jax.random.fold_in(jax.random.fold_in(own_key, 6), dim), (shards_of,), jnp.float32, low / len(cuts), top_value / len(cuts))
        return jnp.repeat(jnp.exp(steps), extent[dim] // shards_of).reshape((-1,) + (1,) * (len(extent) - dim - 1))

    gain = one(*cuts[0])
    for cut in cuts[1:]:
        gain = gain * one(*cut)
    return gain


def bell_draw(stream_key, extent, width, limit, cuts=(), kind=jnp.bfloat16):
    values = width * jax.random.normal(stream_key, extent, jnp.float32)
    if cuts:
        values = values * levels(stream_key, extent, cuts, -0.22, 0.18)
    return jnp.clip(values, -limit, limit).astype(kind)


def heavy_noise(rng, extent, scale, limit, cuts, heavy, kind=jnp.bfloat16):
    entries = scale * jax.random.normal(rng, extent, jnp.float32)
    if cuts:
        entries = entries * levels(rng, extent, cuts, -0.22, 0.18)
    return jnp.clip(raised(entries, jax.random.fold_in(rng, 3), *heavy), -limit, limit).astype(kind)


def setup_inputs(seed: int = 0) -> dict:
    splits = jax.random.split(jax.random.key(seed), 31)
    text = bell_draw(splits[0], (ITEMS, SEQ, D), 1.0, 6.0, ((0, 32),))
    lengths = draw_lengths(jax.random.fold_in(splits[30], 71), 0)
    patches = bell_draw(splits[2], (ITEMS, NP, VW), 1.0, 6.0, ((0, 32),))
    w_query = bell_draw(splits[3], (D, D), D ** -0.5, 0.21875, ((0, 32),))
    w_key = bell_draw(splits[4], (D, D), D ** -0.5, 0.21875, ((0, 32),))
    w_value = bell_draw(splits[5], (D, D), D ** -0.5, 0.21875, ((0, 32),))
    w_out = bell_draw(splits[6], (D, D), (D // 8) ** -0.5, 0.625, ((0, 32),))
    b_query = bell_draw(splits[7], (D,), 0.5, 3.0, (), jnp.float32)
    b_value = bell_draw(splits[8], (D,), 0.5, 3.0, (), jnp.float32)
    b_out = bell_draw(splits[9], (D,), 0.5, 3.0, (), jnp.float32)
    gain_one = jnp.clip(1.0 + 0.1 * jax.random.normal(splits[10], (D,), jnp.float32), 0.5, 1.5)
    bias_one = bell_draw(splits[11], (D,), 0.5, 3.0, (), jnp.float32)
    w_image = bell_draw(splits[12], (VW, D), VW ** -0.5, 0.1875, ((0, 32),))
    b_image = bell_draw(splits[13], (D,), 0.5, 3.0, (), jnp.float32)
    c_query = bell_draw(splits[14], (D, D), D ** -0.5, 0.21875, ((0, 32),))
    c_key = bell_draw(splits[15], (D, D), D ** -0.5, 0.21875, ((0, 32),))
    c_value = bell_draw(splits[16], (D, D), D ** -0.5, 0.21875, ((0, 32),))
    c_out = bell_draw(splits[17], (D, D), (D // 16) ** -0.5, 0.875, ((0, 32),))
    cb_query = bell_draw(splits[18], (D,), 0.5, 3.0, (), jnp.float32)
    cb_value = bell_draw(splits[19], (D,), 0.5, 3.0, (), jnp.float32)
    cb_out = bell_draw(splits[20], (D,), 0.5, 3.0, (), jnp.float32)
    gain_two = jnp.clip(1.0 + 0.1 * jax.random.normal(splits[21], (D,), jnp.float32), 0.5, 1.5)
    bias_two = bell_draw(splits[22], (D,), 0.5, 3.0, (), jnp.float32)
    w_inner = bell_draw(splits[23], (D, FF), D ** -0.5, 0.21875, ((0, 32),))
    b_inner = bell_draw(splits[24], (FF,), 0.5, 3.0, (), jnp.float32)
    w_outer = bell_draw(splits[25], (FF, D), (FF // 4) ** -0.5, 0.21875, ((0, 32),))
    b_outer = bell_draw(splits[26], (D,), 0.5, 3.0, (), jnp.float32)
    gain_three = jnp.clip(1.0 + 0.1 * jax.random.normal(splits[27], (D,), jnp.float32), 0.5, 1.5)
    bias_three = bell_draw(splits[28], (D,), 0.5, 3.0, (), jnp.float32)
    cotangent = heavy_noise(splits[29], (ITEMS, SEQ, D), 1.0, 6.0, ((0, 32),), (0, 2, 32, 2.75))
    return dict(text=text, lengths=lengths, patches=patches, w_query=w_query, w_key=w_key, w_value=w_value, w_out=w_out, b_query=b_query, b_value=b_value, b_out=b_out, gain_one=gain_one, bias_one=bias_one, w_image=w_image, b_image=b_image, c_query=c_query, c_key=c_key, c_value=c_value, c_out=c_out, cb_query=cb_query, cb_value=cb_value, cb_out=cb_out, gain_two=gain_two, bias_two=bias_two, w_inner=w_inner, b_inner=b_inner, w_outer=w_outer, b_outer=b_outer, gain_three=gain_three, bias_three=bias_three, cotangent=cotangent)


highest = lax.Precision.HIGHEST
neg_large = -1000000000.0
ln_eps = 1e-06

@jax.custom_vjp
def low(v):
    return lax.optimization_barrier(v.astype(jnp.bfloat16)).astype(jnp.float32)

@jax.custom_vjp
def low_back(v):
    return v

def low_keep(v):
    return (low(v), None)

def low_pass(kept, grad):
    return (grad,)

def back_keep(v):
    return (v, None)

def back_low(kept, grad):
    return (low(grad),)
low.defvjp(low_keep, low_pass)
low_back.defvjp(back_keep, back_low)

def matmul(left_rows, right_mat):
    return jnp.dot(left_rows, right_mat, precision=highest)

def layer_norm(values, gain_vec, shift_vec):
    centered = values - lax.optimization_barrier(jnp.mean(values, axis=-1, keepdims=True))
    spread = lax.optimization_barrier(jnp.mean(centered * centered, axis=-1, keepdims=True))
    return centered * lax.rsqrt(spread + ln_eps) * gain_vec + shift_vec

def rounded(values):
    return low_back(low(values))

def split_heads(values, item_count):
    return values.reshape(item_count, -1, HEADS, HEAD_DIM)

def attend(query_rows, key_rows, value_rows, mask_bias):
    scores = jnp.einsum('bqhe,bkhe->bhqk', query_rows, key_rows, precision=highest)
    scores = low_back(scores * HEAD_DIM ** (-0.5) + mask_bias)
    row_top = lax.optimization_barrier(jnp.max(scores, axis=-1, keepdims=True))
    weights = jnp.exp(scores - row_top)
    probs_full = low(weights / lax.optimization_barrier(jnp.sum(weights, axis=-1, keepdims=True)))
    return jnp.einsum('bhqk,bkhe->bqhe', probs_full, value_rows, precision=highest)

def forward(text, images, params, keep_mask):
    w_query, w_key, w_value, w_out, b_query, b_value, b_out, gain_one, bias_one, w_image, b_image, c_query, c_key, c_value, c_out, cb_query, cb_value, cb_out, gain_two, bias_two, w_inner, b_inner, w_outer, b_outer, gain_three, bias_three = params
    item_count = text.shape[0]
    text_rows = text.reshape(-1, D)
    query_rows = rounded(matmul(text_rows, w_query) + b_query)
    key_rows = rounded(matmul(text_rows, w_key))
    value_rows = rounded(matmul(text_rows, w_value) + b_value)
    mask_bias = jnp.where(keep_mask > 0.5, 0.0, neg_large)[:, None, None, :]
    self_heads = attend(split_heads(query_rows, item_count), split_heads(key_rows, item_count), split_heads(value_rows, item_count), mask_bias)
    attn_rows = rounded(self_heads.reshape(-1, D))
    branch = low_back(matmul(attn_rows, w_out) + b_out)
    hidden = low(layer_norm(text_rows + branch, gain_one, bias_one))
    image_rows = rounded(matmul(images.reshape(-1, VW), w_image) + b_image)
    cross_keys = rounded(matmul(image_rows, c_key))
    cross_values = rounded(matmul(image_rows, c_value) + cb_value)
    cross_query = rounded(matmul(hidden, c_query) + cb_query)
    cross_heads = attend(split_heads(cross_query, item_count), split_heads(cross_keys, item_count), split_heads(cross_values, item_count), 0.0)
    cross_rows = rounded(cross_heads.reshape(-1, D))
    cross_branch = low_back(matmul(cross_rows, c_out) + cb_out)
    joint_rows = low(layer_norm(hidden + cross_branch, gain_two, bias_two))
    inner_pre = low_back(matmul(joint_rows, w_inner) + b_inner)
    active = low(jax.nn.gelu(inner_pre, approximate=False))
    outer_pre = low_back(matmul(active, w_outer) + b_outer)
    result = layer_norm(joint_rows + outer_pre, gain_three, bias_three)
    return result.reshape(item_count, -1, D) * keep_mask[:, :, None]

def reference(text, lengths, patches, w_query, w_key, w_value, w_out, b_query, b_value, b_out, gain_one, bias_one, w_image, b_image, c_query, c_key, c_value, c_out, cb_query, cb_value, cb_out, gain_two, bias_two, w_inner, b_inner, w_outer, b_outer, gain_three, bias_three, cotangent):
    half_items = ITEMS // 2
    images = jnp.concatenate([patches[half_items:], patches[:half_items]], axis=0)
    positions = jnp.arange(SEQ, dtype=jnp.int32)
    keep_mask = (positions[None, :] < lengths[:, None]).astype(jnp.float32)
    params = tuple((member.astype(jnp.float32) for member in (w_query, w_key, w_value, w_out, b_query, b_value, b_out, gain_one, bias_one, w_image, b_image, c_query, c_key, c_value, c_out, cb_query, cb_value, cb_out, gain_two, bias_two, w_inner, b_inner, w_outer, b_outer, gain_three, bias_three)))
    blocks = ITEMS // 32

    def regroup(values):
        return values.reshape((blocks, 32) + values.shape[1:])

    def group_step(totals, pieces):
        text_block, image_block, keep_block, cot_block = pieces

        def local_forward(text_in, image_in, param_in):
            return forward(text_in, image_in, param_in, keep_block)
        result, pullback = jax.vjp(local_forward, text_block.astype(jnp.float32), image_block.astype(jnp.float32), params)
        text_grad, image_grad, param_grad = pullback(cot_block.astype(jnp.float32))
        totals = jax.tree.map(jnp.add, totals, param_grad)
        return (totals, (result, text_grad, image_grad))
    zero_grads = jax.tree.map(jnp.zeros_like, params)
    grad_sums, (mixed_out, grad_text, image_grad) = lax.scan(group_step, zero_grads, (regroup(text), regroup(images), regroup(keep_mask), regroup(cotangent)))
    mixed_out = mixed_out.reshape(ITEMS, SEQ, D)
    grad_text = grad_text.reshape(ITEMS, SEQ, D)
    image_grad = image_grad.reshape(ITEMS, NP, VW)
    grad_patches = jnp.concatenate([image_grad[half_items:], image_grad[:half_items]], axis=0)
    return (mixed_out, grad_text, grad_patches, grad_sums[0], grad_sums[1], grad_sums[2], grad_sums[3], grad_sums[4], grad_sums[5], grad_sums[6], grad_sums[7], grad_sums[8], grad_sums[9], grad_sums[10], grad_sums[11], grad_sums[12], grad_sums[13], grad_sums[14], grad_sums[15], grad_sums[16], grad_sums[17], grad_sums[18], grad_sums[19], grad_sums[20], grad_sums[21], grad_sums[22], grad_sums[23], grad_sums[24], grad_sums[25])
```

```python
import jax
import jax.numpy as jnp
from jax import lax
from jax.experimental import pallas as pl
from jax.experimental.pallas import tpu as pltpu
from jax.sharding import PartitionSpec as P

D = 768
HD = 64
GROUP = 256
NGROUP = 3
PER = 4
VW = 1024
NP = 145
SEQ = 40
ITEMS = 4
TP = 48
IP = 160
TR = ITEMS * TP
IR = ITEMS * IP
FF = 3072
HALF = D // 2
CHIPS = 16
LANES = CHIPS * 2
SCALE = HD**-0.5
neg_large = -1000000000.0
ln_eps = 1e-06
bf16 = jnp.bfloat16
f32 = jnp.float32
AXES = ("mod", "dp")

Y, Z0, Z1, X = 1, 2, 4, 8
ZS = (0, Z0, Z1, Z0 | Z1)


def layout_of(first):
    last = Y if first == X else X
    return [z for z in ZS] + [z ^ first for z in ZS], last


PIECES = {
    "qkv": ((48, 48, 48), X),
    "img": ((64, 48, 48), Y),
    "mid": ((48, 48, 48), X),
    "inner": ((48, 48, 48, 48), Y),
    "outer": ((192,), X),
}


def mm(a, b):
    return jnp.dot(a, b, preferred_element_type=f32)


def mm_t(a, b):
    return lax.dot_general(a, b, (((1,), (1,)), ((), ())), preferred_element_type=f32)


def mm_w(a, b):
    return lax.dot_general(a, b, (((0,), (0,)), ((), ())), preferred_element_type=f32)


def rowsum(a):
    return jnp.sum(a.astype(f32), axis=0, keepdims=True)


def ln_parts(v):
    centered = v - jnp.mean(v, axis=-1, keepdims=True)
    spread = jnp.mean(centered * centered, axis=-1, keepdims=True)
    scale = lax.rsqrt(spread + ln_eps)
    return centered * scale, scale


def ln_back(grad, normed, scale, gain):
    a = grad * gain
    inner = a - jnp.mean(a, axis=-1, keepdims=True)
    return scale * (inner - normed * jnp.mean(a * normed, axis=-1, keepdims=True))


def head_masks():
    head = lax.broadcasted_iota(jnp.int32, (1, GROUP), 1) // HD
    return [jnp.where(head == h, 1.0, 0.0) for h in range(PER)]


def expand(rows, masks):
    return jnp.concatenate([rows * m.astype(bf16) for m in masks], axis=0)


def collapse(full, masks):
    total = full[0:TP] * masks[0]
    for h in range(1, PER):
        total = total + full[h * TP : (h + 1) * TP] * masks[h]
    return total


def softmax_rows(scores):
    e = jnp.exp(scores - jnp.max(scores, axis=-1, keepdims=True))
    return e / jnp.sum(e, axis=-1, keepdims=True)


def attend_forward(q_ref, k_ref, v_ref, o_ref, key_rows, length_of):
    masks = head_masks()
    column = lax.broadcasted_iota(jnp.int32, (1, key_rows), 1)

    def item(i, carry):
        rows = pl.ds(pl.multiple_of(i * TP, 16), TP)
        keys = pl.ds(pl.multiple_of(i * key_rows, 16), key_rows)
        bias = jnp.where(column < length_of(i), 0.0, neg_large)
        for g in range(NGROUP):
            lanes = slice(g * GROUP, (g + 1) * GROUP)
            q = expand(q_ref[rows, lanes], masks)
            probs = softmax_rows(mm_t(q, k_ref[keys, lanes]) * SCALE + bias)
            out = mm(probs.astype(bf16), v_ref[keys, lanes])
            o_ref[rows, lanes] = collapse(out, masks).astype(bf16)
        return carry

    lax.fori_loop(0, ITEMS, item, 0)


def attend_backward(go_ref, q_ref, k_ref, v_ref, dq_ref, dk_ref, dv_ref, key_rows, length_of):
    masks = head_masks()
    column = lax.broadcasted_iota(jnp.int32, (1, key_rows), 1)

    def item(i, carry):
        rows = pl.ds(pl.multiple_of(i * TP, 16), TP)
        keys = pl.ds(pl.multiple_of(i * key_rows, 16), key_rows)
        bias = jnp.where(column < length_of(i), 0.0, neg_large)
        for g in range(NGROUP):
            lanes = slice(g * GROUP, (g + 1) * GROUP)
            q = expand(q_ref[rows, lanes], masks)
            k = k_ref[keys, lanes]
            probs = softmax_rows(mm_t(q, k) * SCALE + bias)
            go = expand(go_ref[rows, lanes], masks)
            dp = mm_t(go, v_ref[keys, lanes])
            ds = (probs * (dp - jnp.sum(probs * dp, axis=-1, keepdims=True))).astype(bf16)
            dq_ref[rows, lanes] = (collapse(mm(ds, k), masks) * SCALE).astype(bf16)
            dk_ref[keys, lanes] = (mm_w(ds, q) * SCALE).astype(bf16)
            dv_ref[keys, lanes] = mm_w(probs.astype(bf16), go).astype(bf16)
        return carry

    lax.fori_loop(0, ITEMS, item, 0)


def piece_kernel(body, piece, grads, meta, ins, outs):
    name, bufs = piece
    sizes, first = PIECES[name]
    rows = sum(sizes)
    base, last = layout_of(first)
    half = len(base)
    n_in, n_out = len(ins), len(outs)

    def kernel(*refs):
        meta_ref, refs = refs[0], refs[1:]
        in_refs, refs = refs[:n_in], refs[n_in:]
        buf_refs, refs = refs[:4], refs[4:]
        out_refs, refs = refs[:n_out], refs[n_out:]
        if grads:
            grad_refs, refs = refs[:4], refs[4:]
            w_ref, load_sem, g_ref, store_sem = refs
        else:
            w_ref, load_sem = refs
        chip, core = meta_ref[0], meta_ref[1]
        columns = [
            pl.ds(pl.multiple_of(core * HALF, 128), HALF),
            pl.ds(pl.multiple_of((1 - core) * HALF, 128), HALF),
        ]

        def copies(hbm, vmem, sem, out):
            made = []
            for side in range(2):
                for part in range(2):
                    for j in range(half):
                        at = chip ^ (base[j] ^ (last if part else 0))
                        outside = hbm[side * 2 + part].at[j]
                        inside = vmem.at[at, :, columns[side]]
                        pair = (inside, outside) if out else (outside, inside)
                        made.append(pltpu.make_async_copy(*pair, sem.at[len(made)]))
            return made

        loads = copies(buf_refs, w_ref, load_sem, False)
        for copy in loads:
            copy.start()

        def ready():
            for copy in loads:
                copy.wait()

        def weight(k):
            low = sum(sizes[:k])
            return w_ref[:, low : low + sizes[k], :].reshape(CHIPS * sizes[k], D)

        def put(k, value):
            low = sum(sizes[:k])
            g_ref[:, low : low + sizes[k], :] = value.astype(bf16).reshape(CHIPS, sizes[k], D)

        body(meta_ref, ready, weight, put, in_refs, out_refs)
        if grads:
            stores = copies(grad_refs, g_ref, store_sem, True)
            for copy in stores:
                copy.start()
            for copy in stores:
                copy.wait()

    vmem = pl.BlockSpec(memory_space=pltpu.VMEM)
    hbm = pl.BlockSpec(memory_space=pl.ANY)
    out_shape = list(outs)
    out_specs = [vmem] * n_out
    scratch = [pltpu.VMEM((CHIPS, rows, D), bf16), pltpu.SemaphoreType.DMA((4 * half,))]
    if grads:
        out_shape += [jax.ShapeDtypeStruct((half, rows, HALF), bf16)] * 4
        out_specs += [hbm] * 4
        scratch += [pltpu.VMEM((CHIPS, rows, D), bf16), pltpu.SemaphoreType.DMA((4 * half,))]
    return pl.pallas_call(
        kernel,
        out_shape=out_shape,
        in_specs=[pl.BlockSpec(memory_space=pltpu.SMEM)] + [vmem] * n_in + [hbm] * 4,
        out_specs=out_specs,
        scratch_shapes=scratch,
        compiler_params=pltpu.CompilerParams(vmem_limit_bytes=48 * 1024 * 1024),
        name=name + ("_back" if grads else "_front"),
    )(meta, *ins, *bufs)


def shape(*dims, dtype=bf16):
    return jax.ShapeDtypeStruct(dims, dtype)


def self_front(meta, ready, weight, put, ins, outs):
    text, b_query, b_value = ins
    q, k, v, attn = outs
    ready()
    rows = text[...]
    q[...] = (mm(rows, weight(0)) + b_query[...]).astype(bf16)
    k[...] = mm(rows, weight(1)).astype(bf16)
    v[...] = (mm(rows, weight(2)) + b_value[...]).astype(bf16)
    attend_forward(q, k, v, attn, TP, lambda i: meta[2 + i])


def image_front(meta, ready, weight, put, ins, outs):
    images, b_image, cb_value = ins
    image_rows, ck, cv = outs
    ready()
    image_rows[...] = (mm(images[...], weight(0)) + b_image[...]).astype(bf16)
    ck[...] = mm(image_rows[...], weight(1)).astype(bf16)
    cv[...] = (mm(image_rows[...], weight(2)) + cb_value[...]).astype(bf16)


def mid_front(meta, ready, weight, put, ins, outs):
    text, attn, ck, cv, b_out, gain_one, bias_one, cb_query, cb_out, gain_two, bias_two = ins
    hidden, cq, cross, joint, sum_one, sum_two = outs
    ready()
    sum_one[...] = text[...].astype(f32) + (mm(attn[...], weight(0)) + b_out[...])
    normed, _ = ln_parts(sum_one[...])
    hidden[...] = (normed * gain_one[...] + bias_one[...]).astype(bf16)
    cq[...] = (mm(hidden[...], weight(1)) + cb_query[...]).astype(bf16)
    attend_forward(cq, ck, cv, cross, IP, lambda i: NP)
    sum_two[...] = hidden[...].astype(f32) + (mm(cross[...], weight(2)) + cb_out[...])
    normed, _ = ln_parts(sum_two[...])
    joint[...] = (normed * gain_two[...] + bias_two[...]).astype(bf16)


def inner_front(meta, ready, weight, put, ins, outs):
    joint, b_inner = ins
    active, slope = outs
    ready()
    for k in range(4):
        lanes = slice(k * D, (k + 1) * D)
        pre = mm(joint[...], weight(k)) + b_inner[:, lanes]
        cdf = 0.5 * (1.0 + lax.erf(pre * 0.5**0.5))
        active[:, lanes] = (pre * cdf).astype(bf16)
        slope[:, lanes] = cdf + pre * (jnp.exp(-0.5 * pre * pre) * 0.3989422804014327)


def outer_both(meta, ready, weight, put, ins, outs):
    active, slope, joint, cot, b_outer, gain, bias = ins
    mixed, grad_sum, grad_inner, vec = outs
    ready()
    normed, scale = ln_parts(joint[...].astype(f32) + (mm(active[...], weight(0)) + b_outer[...]))
    result = normed * gain[...] + bias[...]
    row = lax.broadcasted_iota(jnp.int32, (TP, 1), 0)
    keep = [jnp.where(row < meta[2 + i], 1.0, 0.0) for i in range(ITEMS)]
    for i in range(ITEMS):
        mixed[i] = (result[i * TP : (i + 1) * TP] * keep[i])[:SEQ]
    grad = cot[...].astype(f32) * jnp.concatenate(keep, axis=0)
    grad_sum[...] = ln_back(grad, normed, scale, gain[...])
    grad_outer = grad_sum[...].astype(bf16)
    vec[0:1] = rowsum(grad * normed)
    vec[1:2] = rowsum(grad)
    vec[2:3] = rowsum(grad_outer)
    vec[3:4] = jnp.zeros((1, D), f32)
    put(0, mm_w(active[...], grad_outer))
    for k in range(4):
        lanes = slice(k * D, (k + 1) * D)
        back = mm_t(grad_outer, weight(0)[k * D : (k + 1) * D])
        part = (slope[:, lanes] * back).astype(bf16)
        grad_inner[:, lanes] = part
        vec[4 + k : 5 + k] = rowsum(part)


def inner_back(meta, ready, weight, put, ins, outs):
    joint, grad_inner, grad_sum_three, sum_two, gain = ins
    grad_sum_two, vec = outs
    for k in range(4):
        put(k, mm_w(joint[...], grad_inner[:, k * D : (k + 1) * D]))
    ready()
    grad = grad_sum_three[...]
    for k in range(4):
        grad = grad + mm_t(grad_inner[:, k * D : (k + 1) * D], weight(k))
    normed, scale = ln_parts(sum_two[...])
    grad_sum_two[...] = ln_back(grad, normed, scale, gain[...])
    vec[...] = jnp.concatenate([rowsum(grad * normed), rowsum(grad), jnp.zeros((6, D), f32)], axis=0)


def mid_back(meta, ready, weight, put, ins, outs):
    grad_sum_two, cross, hidden, attn, cq, ck, cv, sum_one, gain = ins
    grad_sum_one, grad_attn, dk, dv, dq, vec = outs
    grad_cross_branch = grad_sum_two[...].astype(bf16)
    put(2, mm_w(cross[...], grad_cross_branch))
    ready()
    grad_attn[...] = mm_t(grad_cross_branch, weight(2)).astype(bf16)
    attend_backward(grad_attn, cq, ck, cv, dq, dk, dv, IP, lambda i: NP)
    put(1, mm_w(hidden[...], dq[...]))
    grad = grad_sum_two[...] + mm_t(dq[...], weight(1))
    normed, scale = ln_parts(sum_one[...])
    grad_sum_one[...] = ln_back(grad, normed, scale, gain[...])
    grad_branch = grad_sum_one[...].astype(bf16)
    put(0, mm_w(attn[...], grad_branch))
    grad_attn[...] = mm_t(grad_branch, weight(0)).astype(bf16)
    vec[...] = jnp.concatenate(
        [
            rowsum(grad_cross_branch),
            rowsum(dq[...]),
            rowsum(grad * normed),
            rowsum(grad),
            rowsum(grad_branch),
            jnp.zeros((3, D), f32),
        ],
        axis=0,
    )


def image_back(meta, ready, weight, put, ins, outs):
    images, image_rows, dk, dv = ins
    grad_patches, vec = outs
    put(1, mm_w(image_rows[...], dk[...]))
    put(2, mm_w(image_rows[...], dv[...]))
    ready()
    grad_image = (mm_t(dk[...], weight(1)) + mm_t(dv[...], weight(2))).astype(bf16)
    put(0, mm_w(images[...], grad_image))
    for i in range(ITEMS):
        grad_patches[i] = mm_t(grad_image[i * IP : (i + 1) * IP], weight(0))[:NP]
    vec[...] = jnp.concatenate([rowsum(dv[...]), rowsum(grad_image), jnp.zeros((6, D), f32)], axis=0)


def self_back(meta, ready, weight, put, ins, outs):
    grad_attn, q, k, v, text, grad_sum_one = ins
    grad_text, dq, dk, dv, vec = outs
    attend_backward(grad_attn, q, k, v, dq, dk, dv, TP, lambda i: meta[2 + i])
    put(0, mm_w(text[...], dq[...]))
    put(1, mm_w(text[...], dk[...]))
    put(2, mm_w(text[...], dv[...]))
    ready()
    total = grad_sum_one[...] + mm_t(dq[...], weight(0))
    total = total + mm_t(dk[...], weight(1))
    grad_text[...] = (total + mm_t(dv[...], weight(2))).astype(bf16)
    vec[...] = jnp.concatenate([rowsum(dq[...]), rowsum(dv[...]), jnp.zeros((6, D), f32)], axis=0)


def local(
    text,
    lengths,
    patches,
    w_query,
    w_key,
    w_value,
    w_out,
    b_query,
    b_value,
    b_out,
    gain_one,
    bias_one,
    w_image,
    b_image,
    c_query,
    c_key,
    c_value,
    c_out,
    cb_query,
    cb_value,
    cb_out,
    gain_two,
    bias_two,
    w_inner,
    b_inner,
    w_outer,
    b_outer,
    gain_three,
    bias_three,
    cotangent,
):
    count = lax.axis_size("mod") * lax.axis_size("dp")
    fold = count // LANES
    device = lax.axis_index("mod") * lax.axis_size("dp") + lax.axis_index("dp")
    place = device // fold
    core, chip = place % 2, place // 2
    first_core = core == 0

    def flip_device(block, mask):
        return lax.ppermute(block, AXES, [(i, i ^ mask) for i in range(count)])

    def flip_chip(block, mask):
        return flip_device(block, mask * 2 * fold)

    def flip_core(block):
        return flip_device(block, fold)

    def swap(block):
        return lax.ppermute(block, "mod", [(0, 1), (1, 0)])

    def gather_fold(shard):
        step = 1
        while step < fold:
            other = flip_device(shard, step)
            low = (device // step) % 2 == 0
            shard = jnp.concatenate(
                [jnp.where(low, shard, other), jnp.where(low, other, shard)], axis=0
            )
            step *= 2
        return shard

    def scatter_fold(total):
        step = fold // 2
        while step >= 1:
            low = (device // step) % 2 == 0
            half = total.shape[0] // 2
            kept = jnp.where(low, total[:half], total[half:])
            total = kept + flip_device(jnp.where(low, total[half:], total[:half]), step)
            step //= 2
        return total

    def gather_piece(name, shards):
        sizes, first = PIECES[name]
        shards = [gather_fold(s) for s in shards]
        lows, highs = [s[:, :HALF] for s in shards], [s[:, HALF:] for s in shards]
        kept = [jnp.where(first_core, a, b) for a, b in zip(lows, highs)]
        sent = jnp.concatenate([jnp.where(first_core, b, a) for a, b in zip(lows, highs)], axis=0)
        came = flip_core(sent)
        parts, at = [], 0
        for mine, size in zip(kept, sizes):
            theirs = came[at : at + size // 2]
            at += size // 2
            parts += [jnp.where(first_core, mine, theirs), jnp.where(first_core, theirs, mine)]
        block = jnp.concatenate(parts, axis=0)
        blocks = jnp.stack([block] + [flip_chip(block, z) for z in ZS[1:]])
        _, last = layout_of(first)
        own_0 = jnp.concatenate([blocks, flip_chip(blocks, first)], axis=0)
        own_1 = flip_chip(own_0, last)
        return name, (own_0, own_1, flip_core(own_0), flip_core(own_1))

    def reduce_piece(name, bufs):
        sizes, first = PIECES[name]
        _, last = layout_of(first)
        keep_0, keep_1, send_0, send_1 = bufs
        came_1 = flip_core(send_1)
        came_0 = flip_core(send_0)
        far = flip_chip((keep_1.astype(f32) + came_1.astype(f32)).astype(bf16), last)
        near = keep_0.astype(f32) + came_0.astype(f32) + far.astype(f32)
        across = flip_chip(near[4:].astype(bf16), first)
        blocks = (near[:4] + across.astype(f32)).astype(bf16)
        total = blocks[0].astype(f32)
        for j in range(1, 4):
            total = total + flip_chip(blocks[j], ZS[j]).astype(f32)
        at, mine, theirs = 0, [], []
        for size in sizes:
            a, b = total[at : at + size // 2], total[at + size // 2 : at + size]
            mine.append(jnp.where(first_core, a, b))
            theirs.append(jnp.where(first_core, b, a))
            at += size
        came = flip_core(jnp.concatenate(theirs, axis=0))
        result, at = [], 0
        for part in mine:
            other = came[at : at + part.shape[0]]
            at += part.shape[0]
            joined = [jnp.where(first_core, part, other), jnp.where(first_core, other, part)]
            result.append(scatter_fold(jnp.concatenate(joined, axis=1)))
        return result

    def sum_all(total):
        step = 1
        while step < 2 * fold * Y * 2:
            total = total + flip_device(total, step)
            step *= 2
        total = total + flip_chip(total, X)
        return total + flip_chip(total, Z0) + (flip_chip(total, Z1) + flip_chip(total, Z0 | Z1))

    def row(vector):
        return vector.reshape(1, -1)

    text_rows = swap(jnp.pad(text, ((0, 0), (0, TP - SEQ), (0, 0))).reshape(TR, D))
    item_lengths = swap(lengths)
    meta = jnp.concatenate([chip[None], core[None], item_lengths]).astype(jnp.int32)
    qkv = gather_piece("qkv", [w_query, w_key, w_value])
    img = gather_piece("img", [w_image, c_key, c_value])
    mid = gather_piece("mid", [w_out, c_query, c_out])
    inner = gather_piece("inner", [w_inner[:, k * D : (k + 1) * D] for k in range(4)])
    outer = gather_piece("outer", [w_outer])
    cot_rows = swap(jnp.pad(cotangent, ((0, 0), (0, TP - SEQ), (0, 0))).reshape(TR, D))
    images = jnp.pad(patches, ((0, 0), (0, IP - NP), (0, 0))).reshape(IR, VW)

    text_shape, image_shape = shape(TR, D), shape(IR, D)
    wide = shape(TR, D, dtype=f32)
    vec_shape = shape(8, D, dtype=f32)
    q, k, v, attn = piece_kernel(
        self_front, qkv, False, meta, [text_rows, row(b_query), row(b_value)], [text_shape] * 4
    )
    image_rows, ck, cv = piece_kernel(
        image_front, img, False, meta, [images, row(b_image), row(cb_value)], [image_shape] * 3
    )
    mid_params = [b_out, gain_one, bias_one, cb_query, cb_out, gain_two, bias_two]
    hidden, cq, cross, joint, sum_one, sum_two = piece_kernel(
        mid_front,
        mid,
        False,
        meta,
        [text_rows, attn, ck, cv] + [row(p) for p in mid_params],
        [text_shape] * 4 + [wide] * 2,
    )
    active, slope = piece_kernel(
        inner_front,
        inner,
        False,
        meta,
        [joint, row(b_inner)],
        [shape(TR, FF), shape(TR, FF, dtype=f32)],
    )
    mixed, grad_sum_three, grad_inner, vec_outer, *outer_grads = piece_kernel(
        outer_both,
        outer,
        True,
        meta,
        [active, slope, joint, cot_rows, row(b_outer), row(gain_three), row(bias_three)],
        [shape(ITEMS, SEQ, D, dtype=f32), wide, shape(TR, FF), vec_shape],
    )
    mixed_out = swap(mixed)
    (grad_w_outer,) = reduce_piece("outer", outer_grads)
    grad_sum_two, vec_inner, *inner_grads = piece_kernel(
        inner_back,
        inner,
        True,
        meta,
        [joint, grad_inner, grad_sum_three, sum_two, row(gain_two)],
        [wide, vec_shape],
    )
    grad_w_inner = jnp.concatenate(reduce_piece("inner", inner_grads), axis=1)
    grad_sum_one, grad_attn, dk, dv, _, vec_mid, *mid_grads = piece_kernel(
        mid_back,
        mid,
        True,
        meta,
        [grad_sum_two, cross, hidden, attn, cq, ck, cv, sum_one, row(gain_one)],
        [wide, text_shape, image_shape, image_shape, text_shape, vec_shape],
    )
    grad_w_out, grad_c_query, grad_c_out = reduce_piece("mid", mid_grads)
    grad_patches, vec_image, *img_grads = piece_kernel(
        image_back,
        img,
        True,
        meta,
        [images, image_rows, dk, dv],
        [shape(ITEMS, NP, VW, dtype=f32), vec_shape],
    )
    grad_w_image, grad_c_key, grad_c_value = reduce_piece("img", img_grads)
    grad_text, _, _, _, vec_self, *qkv_grads = piece_kernel(
        self_back,
        qkv,
        True,
        meta,
        [grad_attn, q, k, v, text_rows, grad_sum_one],
        [text_shape] * 4 + [vec_shape],
    )
    grad_w_query, grad_w_key, grad_w_value = reduce_piece("qkv", qkv_grads)
    grad_text = swap(grad_text).reshape(ITEMS, TP, D)[:, :SEQ].astype(f32)
    vecs = sum_all(jnp.concatenate([vec_outer, vec_inner, vec_mid, vec_image, vec_self], axis=0))
    grad_b_inner = vecs[4:8].reshape(FF)
    return (
        mixed_out,
        grad_text,
        grad_patches,
        grad_w_query,
        grad_w_key,
        grad_w_value,
        grad_w_out,
        vecs[32],
        vecs[33],
        vecs[20],
        vecs[18],
        vecs[19],
        grad_w_image,
        vecs[25],
        grad_c_query,
        grad_c_key,
        grad_c_value,
        grad_c_out,
        vecs[17],
        vecs[24],
        vecs[16],
        vecs[8],
        vecs[9],
        grad_w_inner,
        grad_b_inner,
        grad_w_outer,
        vecs[2],
        vecs[0],
        vecs[1],
    )


def solution(mesh):
    items = P(AXES, None, None)
    shard, whole = P(AXES, None), P()
    in_specs = (
        (items, P(AXES), items)
        + (shard,) * 4
        + (whole,) * 5
        + (shard, whole)
        + (shard,) * 4
        + (whole,) * 5
        + (shard, whole, shard)
        + (whole,) * 3
        + (items,)
    )
    out_specs = (
        (items,) * 3
        + (shard,) * 4
        + (whole,) * 5
        + (shard, whole)
        + (shard,) * 4
        + (whole,) * 5
        + (shard, whole, shard)
        + (whole,) * 3
    )
    return jax.shard_map(local, mesh=mesh, in_specs=in_specs, out_specs=out_specs, check_vma=False)
```

```python
import jax
import jax.numpy as jnp
from jax import lax
from jax.experimental import pallas as pl
from jax.experimental.pallas import tpu as pltpu
from jax.sharding import PartitionSpec as P

D = 768
HD = 64
GROUP = 256
NGROUP = 3
PER = 4
VW = 1024
NP = 145
SEQ = 40
ITEMS = 4
TP = 48
IP = 160
TR = ITEMS * TP
IR = ITEMS * IP
FF = 3072
HALF = D // 2
CHIPS = 16
LANES = CHIPS * 2
SCALE = HD**-0.5
neg_large = -1000000000.0
ln_eps = 1e-06
bf16 = jnp.bfloat16
f32 = jnp.float32
AXES = ("mod", "dp")
MICRO = 1.1e9

Y, Z0, Z1, X = 1, 2, 4, 8
ZS = (0, Z0, Z1, Z0 | Z1)


def held_by(*masks):
    held = [0]
    for group in masks:
        held += [h ^ m for m in group for h in held]
    return held


PACKS = {
    "a": (ZS[1:], (X,), (Y,)),
    "b": (ZS[1:], (Y,), (X,)),
    "ia": ((X,), ZS[1:], (Y,)),
    "ib": ((Y,), ZS[1:], (X,)),
}


def mm(a, b):
    return jnp.dot(a, b, preferred_element_type=f32)


def mm_t(a, b):
    return lax.dot_general(a, b, (((1,), (1,)), ((), ())), preferred_element_type=f32)


def mm_w(a, b):
    return lax.dot_general(a, b, (((0,), (0,)), ((), ())), preferred_element_type=f32)


def rowsum(a):
    return jnp.sum(a.astype(f32), axis=0, keepdims=True)


def ln_parts(v):
    centered = v - jnp.mean(v, axis=-1, keepdims=True)
    spread = jnp.mean(centered * centered, axis=-1, keepdims=True)
    scale = lax.rsqrt(spread + ln_eps)
    return centered * scale, scale


def ln_back(grad, normed, scale, gain):
    a = grad * gain
    inner = a - jnp.mean(a, axis=-1, keepdims=True)
    return scale * (inner - normed * jnp.mean(a * normed, axis=-1, keepdims=True))


def head_masks():
    head = lax.broadcasted_iota(jnp.int32, (1, GROUP), 1) // HD
    return [jnp.where(head == h, 1.0, 0.0) for h in range(PER)]


def expand(rows, masks):
    return jnp.concatenate([rows * m.astype(bf16) for m in masks], axis=0)


def collapse(full, masks):
    total = full[0:TP] * masks[0]
    for h in range(1, PER):
        total = total + full[h * TP : (h + 1) * TP] * masks[h]
    return total


def softmax_rows(scores):
    e = jnp.exp(scores - jnp.max(scores, axis=-1, keepdims=True))
    return e / jnp.sum(e, axis=-1, keepdims=True)


def attend_forward(q_ref, k_ref, v_ref, o_ref, key_rows, length_of):
    masks = head_masks()
    column = lax.broadcasted_iota(jnp.int32, (1, key_rows), 1)

    def item(i, carry):
        rows = pl.ds(pl.multiple_of(i * TP, 16), TP)
        keys = pl.ds(pl.multiple_of(i * key_rows, 16), key_rows)
        bias = jnp.where(column < length_of(i), 0.0, neg_large)
        for g in range(NGROUP):
            lanes = slice(g * GROUP, (g + 1) * GROUP)
            q = expand(q_ref[rows, lanes], masks)
            probs = softmax_rows(mm_t(q, k_ref[keys, lanes]) * SCALE + bias)
            out = mm(probs.astype(bf16), v_ref[keys, lanes])
            o_ref[rows, lanes] = collapse(out, masks).astype(bf16)
        return carry

    lax.fori_loop(0, ITEMS, item, 0, unroll=True)


def attend_backward(go_ref, q_ref, k_ref, v_ref, dq_ref, dk_ref, dv_ref, key_rows, length_of):
    masks = head_masks()
    column = lax.broadcasted_iota(jnp.int32, (1, key_rows), 1)

    def item(i, carry):
        rows = pl.ds(pl.multiple_of(i * TP, 16), TP)
        keys = pl.ds(pl.multiple_of(i * key_rows, 16), key_rows)
        bias = jnp.where(column < length_of(i), 0.0, neg_large)
        for g in range(NGROUP):
            lanes = slice(g * GROUP, (g + 1) * GROUP)
            q = expand(q_ref[rows, lanes], masks)
            k = k_ref[keys, lanes]
            probs = softmax_rows(mm_t(q, k) * SCALE + bias)
            go = expand(go_ref[rows, lanes], masks)
            dp = mm_t(go, v_ref[keys, lanes])
            ds = (probs * (dp - jnp.sum(probs * dp, axis=-1, keepdims=True))).astype(bf16)
            dq_ref[rows, lanes] = (collapse(mm(ds, k), masks) * SCALE).astype(bf16)
            dk_ref[keys, lanes] = (mm_w(ds, q) * SCALE).astype(bf16)
            dv_ref[keys, lanes] = mm_w(probs.astype(bf16), go).astype(bf16)
        return carry

    lax.fori_loop(0, ITEMS, item, 0, unroll=True)


def whole_block(x):
    zeros = (0,) * len(x.shape)
    return pl.BlockSpec(x.shape, lambda i: zeros, pipeline_mode=pl.Buffered(1))


def piece_kernel(body, name, micros, meta, weights, sizes, grads, ins, outs, far=()):
    rows = sum(sizes)
    far_in, far_out, far_scratch = far or ((), (), ())
    n_in, n_out = len(ins), len(outs)
    hbm_in = [buf for _, bufs, _, _ in weights for buf in bufs]
    n_buf = len(hbm_in)
    grad_shapes = [shape(CHIPS, rows, HALF)] * 2 if grads else []
    n_grad = len(grad_shapes)

    def kernel(*refs):
        meta_ref, refs = refs[0], refs[1:]
        in_refs, refs = refs[:n_in], refs[n_in:]
        buf_refs, refs = refs[:n_buf], refs[n_buf:]
        far_refs, refs = refs[: len(far_in)], refs[len(far_in) :]
        out_refs, refs = refs[:n_out], refs[n_out:]
        grad_refs, refs = refs[:n_grad], refs[n_grad:]
        far_refs, refs = far_refs + refs[: len(far_out)], refs[len(far_out) :]
        far_refs, refs = far_refs + refs[: len(far_scratch)], refs[len(far_scratch) :]
        if weights:
            (w_ref, load_sem), refs = refs[:2], refs[2:]
        if grads:
            g_ref, store_sem = refs
        chip, core = meta_ref[0], meta_ref[1]
        columns = [
            pl.ds(pl.multiple_of(core * HALF, 128), HALF),
            pl.ds(pl.multiple_of((1 - core) * HALF, 128), HALF),
        ]

        def copies(groups, vmem, sem, out):
            made, at = [], 0
            for pack, bufs, first, count in groups:
                masks = held_by(*PACKS[pack])
                for side in range(2):
                    for j, mask in enumerate(masks):
                        if out:
                            outside = bufs[side].at[j, first : first + count, :]
                        else:
                            source = bufs[side * 2 + j // 8]
                            outside = source.at[j % 8, first : first + count, :]
                        inside = vmem.at[chip ^ mask, at : at + count, columns[side]]
                        pair = (inside, outside) if out else (outside, inside)
                        made.append(pltpu.make_async_copy(*pair, sem.at[len(made)]))
                at += count
            return made

        loads = []
        if weights:
            groups = [
                (w[0], buf_refs[4 * i : 4 * i + 4], w[2], w[3]) for i, w in enumerate(weights)
            ]
            loads = copies(groups, w_ref, load_sem, False)
        for copy in loads:
            copy.start()

        def ready(group):
            for copy in loads[group * LANES : (group + 1) * LANES]:
                copy.wait()

        def weight(k):
            low = sum(sizes[:k])
            return w_ref[:, low : low + sizes[k], :].reshape(CHIPS * sizes[k], D)

        def put(k, value):
            low = sum(sizes[:k])
            g_ref[:, low : low + sizes[k], :] = value.astype(bf16).reshape(CHIPS, sizes[k], D)

        body(meta_ref, ready, weight, put, in_refs, out_refs + far_refs)
        if grads:
            groups, at = [], 0
            for pack, count in grads:
                groups.append((pack, grad_refs, at, count))
                at += count
            stores = copies(groups, g_ref, store_sem, True)
            for copy in stores:
                copy.start()
            for copy in stores:
                copy.wait()

    hbm = pl.BlockSpec(memory_space=pl.ANY)
    scratch = list(far_scratch)
    if weights:
        scratch += [
            pltpu.VMEM((CHIPS, rows, D), bf16),
            pltpu.SemaphoreType.DMA((LANES * len(weights),)),
        ]
    if grads:
        scratch += [
            pltpu.VMEM((CHIPS, rows, D), bf16),
            pltpu.SemaphoreType.DMA((LANES * len(grads),)),
        ]
    made = pl.pallas_call(
        kernel,
        out_shape=list(outs) + grad_shapes + list(far_out),
        grid=(1,),
        in_specs=[pl.BlockSpec(memory_space=pltpu.SMEM)]
        + [whole_block(x) for x in ins]
        + [hbm] * (n_buf + len(far_in)),
        out_specs=[whole_block(x) for x in outs] + [hbm] * (n_grad + len(far_out)),
        scratch_shapes=scratch,
        compiler_params=pltpu.CompilerParams(vmem_limit_bytes=50 * 1024 * 1024),
        cost_estimate=pl.CostEstimate(
            flops=int(micros * MICRO), bytes_accessed=0, transcendentals=0
        ),
        name=name,
    )(meta, *ins, *hbm_in, *far_in)
    return made[:n_out], made[n_out:]


PARAMS = (
    "b_query b_value b_out gain_one bias_one b_image cb_query".split()
    + "cb_value cb_out gain_two bias_two b_outer gain_three bias_three".split()
)
B_INNER = 16


def param(ref, name):
    at = PARAMS.index(name)
    return ref[at : at + 1]


def join_params(*vectors):
    def kernel(*refs):
        out = refs[-1]
        for i, ref in enumerate(refs[:-2]):
            out[i : i + 1] = ref[...].reshape(1, D)
        out[len(PARAMS) : B_INNER] = jnp.zeros((B_INNER - len(PARAMS), D), f32)
        inner = refs[-2][...].reshape(1, FF)
        for k in range(4):
            out[B_INNER + k : B_INNER + k + 1] = inner[:, k * D : (k + 1) * D]
        out[B_INNER + 4 :] = jnp.zeros((4, D), f32)

    vmem = pl.BlockSpec(memory_space=pltpu.VMEM)
    return pl.pallas_call(
        kernel,
        out_shape=shape(24, D, dtype=f32),
        in_specs=[vmem] * len(vectors),
        out_specs=vmem,
        name="join_params",
    )(*vectors)


def pack_shards(core, shards):
    rows = sum(s.shape[0] * (s.shape[1] // D) for s in shards)

    def kernel(core_ref, *refs):
        parts = []
        for ref in refs[:-2]:
            full = ref[...].astype(f32)
            parts += [full[:, k * D : (k + 1) * D] for k in range(full.shape[1] // D)]
        full = jnp.concatenate(parts, axis=0)
        second = core_ref[0] > 0
        low, high = full[:, :HALF], full[:, HALF:]
        refs[-2][...] = jnp.where(second, high, low).astype(bf16)
        refs[-1][...] = jnp.where(second, low, high).astype(bf16)

    vmem = pl.BlockSpec(memory_space=pltpu.VMEM)
    return pl.pallas_call(
        kernel,
        out_shape=[shape(rows, HALF)] * 2,
        in_specs=[pl.BlockSpec(memory_space=pltpu.SMEM)] + [vmem] * len(shards),
        out_specs=[vmem] * 2,
        name="pack_shards",
    )(core[None].astype(jnp.int32), *shards)


def shape(*dims, dtype=bf16):
    return jax.ShapeDtypeStruct(dims, dtype)


def first_front(meta, ready, weight, put, ins, outs):
    text, images, params = ins
    q, k, v, attn, image_rows, ck, cv = outs
    ready(0)
    rows = text[...]
    q[...] = (mm(rows, weight(0)) + param(params, "b_query")).astype(bf16)
    k[...] = mm(rows, weight(1)).astype(bf16)
    v[...] = (mm(rows, weight(2)) + param(params, "b_value")).astype(bf16)
    attend_forward(q, k, v, attn, TP, lambda i: meta[2 + i])
    ready(1)
    image_rows[...] = (mm(images[...], weight(3)) + param(params, "b_image")).astype(bf16)
    ck[...] = mm(image_rows[...], weight(4)).astype(bf16)
    cv[...] = (mm(image_rows[...], weight(5)) + param(params, "cb_value")).astype(bf16)


def mid_front(meta, ready, weight, put, ins, outs):
    text, attn, ck, cv, params = ins
    hidden, cq, cross, joint, sum_one, sum_two = outs
    ready(0)
    ready(1)
    sum_one[...] = text[...].astype(f32) + (mm(attn[...], weight(0)) + param(params, "b_out"))
    normed, _ = ln_parts(sum_one[...])
    hidden[...] = (normed * param(params, "gain_one") + param(params, "bias_one")).astype(bf16)
    cq[...] = (mm(hidden[...], weight(1)) + param(params, "cb_query")).astype(bf16)
    attend_forward(cq, ck, cv, cross, IP, lambda i: NP)
    sum_two[...] = hidden[...].astype(f32) + (mm(cross[...], weight(2)) + param(params, "cb_out"))
    normed, _ = ln_parts(sum_two[...])
    joint[...] = (normed * param(params, "gain_two") + param(params, "bias_two")).astype(bf16)


def feed_forward(meta, ready, weight, put, ins, outs):
    joint, cot, sum_two, params = ins
    mixed, grad_sum_two, vec_three, vec_two = outs[:4]
    outer_hbm, grad_outer_hbm, outer_w, grad_outer_w, active, slope, grad_inner, sem = outs[4:]
    load = pltpu.make_async_copy(outer_hbm, outer_w, sem.at[0])
    load.start()
    ready(0)
    ready(1)
    for k in range(4):
        lanes = slice(k * D, (k + 1) * D)
        pre = mm(joint[...], weight(k)) + params[B_INNER + k : B_INNER + k + 1]
        cdf = 0.5 * (1.0 + lax.erf(pre * 0.5**0.5))
        active[:, lanes] = (pre * cdf).astype(bf16)
        slope[:, lanes] = cdf + pre * (jnp.exp(-0.5 * pre * pre) * 0.3989422804014327)
    load.wait()
    outer = mm(active[...], outer_w[...]) + param(params, "b_outer")
    normed, scale = ln_parts(joint[...].astype(f32) + outer)
    gain = param(params, "gain_three")
    result = normed * gain + param(params, "bias_three")
    row = lax.broadcasted_iota(jnp.int32, (TP, 1), 0)
    keep = [jnp.where(row < meta[2 + i], 1.0, 0.0) for i in range(ITEMS)]
    for i in range(ITEMS):
        mixed[i] = (result[i * TP : (i + 1) * TP] * keep[i])[:SEQ]
    grad = cot[...].astype(f32) * jnp.concatenate(keep, axis=0)
    grad_sum = ln_back(grad, normed, scale, gain)
    grad_outer = grad_sum.astype(bf16)
    vec_three[0:1] = rowsum(grad * normed)
    vec_three[1:2] = rowsum(grad)
    vec_three[2:3] = rowsum(grad_outer)
    vec_three[3:4] = jnp.zeros((1, D), f32)
    grad_outer_w[...] = mm_w(active[...], grad_outer).astype(bf16)
    store = pltpu.make_async_copy(grad_outer_w, grad_outer_hbm, sem.at[1])
    store.start()
    for k in range(4):
        lanes = slice(k * D, (k + 1) * D)
        part = (slope[:, lanes] * mm_t(grad_outer, outer_w[lanes, :])).astype(bf16)
        grad_inner[:, lanes] = part
        vec_three[4 + k : 5 + k] = rowsum(part)
        put(k, mm_w(joint[...], part))
    grad = grad_sum
    for k in range(4):
        grad = grad + mm_t(grad_inner[:, k * D : (k + 1) * D], weight(k))
    normed, scale = ln_parts(sum_two[...])
    grad_sum_two[...] = ln_back(grad, normed, scale, param(params, "gain_two"))
    vec_two[...] = jnp.concatenate(
        [rowsum(grad * normed), rowsum(grad), jnp.zeros((6, D), f32)], axis=0
    )
    store.wait()


def mid_back(meta, ready, weight, put, ins, outs):
    grad_sum_two, cross, hidden, attn, cq, ck, cv, sum_one, params = ins
    grad_sum_one, grad_attn, dk, dv, vec, dq = outs
    gain = param(params, "gain_one")
    grad_cross_branch = grad_sum_two[...].astype(bf16)
    ready(0)
    ready(1)
    grad_attn[...] = mm_t(grad_cross_branch, weight(2)).astype(bf16)
    attend_backward(grad_attn, cq, ck, cv, dq, dk, dv, IP, lambda i: NP)
    put(2, mm_w(cross[...], grad_cross_branch))
    put(1, mm_w(hidden[...], dq[...]))
    grad = grad_sum_two[...] + mm_t(dq[...], weight(1))
    normed, scale = ln_parts(sum_one[...])
    grad_sum_one[...] = ln_back(grad, normed, scale, gain)
    grad_branch = grad_sum_one[...].astype(bf16)
    put(0, mm_w(attn[...], grad_branch))
    grad_attn[...] = mm_t(grad_branch, weight(0)).astype(bf16)
    vec[...] = jnp.concatenate(
        [
            rowsum(grad_cross_branch),
            rowsum(dq[...]),
            rowsum(grad * normed),
            rowsum(grad),
            rowsum(grad_branch),
            jnp.zeros((3, D), f32),
        ],
        axis=0,
    )


def image_back(meta, ready, weight, put, ins, outs):
    images, image_rows, dk, dv = ins
    grad_patches, vec = outs
    put(1, mm_w(image_rows[...], dk[...]))
    put(2, mm_w(image_rows[...], dv[...]))
    ready(0)
    grad_image = (mm_t(dk[...], weight(1)) + mm_t(dv[...], weight(2))).astype(bf16)
    put(0, mm_w(images[...], grad_image))
    for i in range(ITEMS):
        grad_patches[i] = mm_t(grad_image[i * IP : (i + 1) * IP], weight(0))[:NP]
    vec[...] = jnp.concatenate([rowsum(dv[...]), rowsum(grad_image), jnp.zeros((6, D), f32)], axis=0)


def self_back(meta, ready, weight, put, ins, outs):
    grad_attn, q, k, v, text, grad_sum_one = ins
    grad_text, vec, dq, dk, dv = outs
    attend_backward(grad_attn, q, k, v, dq, dk, dv, TP, lambda i: meta[2 + i])
    put(0, mm_w(text[...], dq[...]))
    put(1, mm_w(text[...], dk[...]))
    put(2, mm_w(text[...], dv[...]))
    ready(0)
    total = grad_sum_one[...] + mm_t(dq[...], weight(0))
    total = total + mm_t(dk[...], weight(1))
    grad_text[...] = (total + mm_t(dv[...], weight(2))).astype(bf16)
    vec[...] = jnp.concatenate([rowsum(dq[...]), rowsum(dv[...]), jnp.zeros((6, D), f32)], axis=0)


def local(
    text,
    lengths,
    patches,
    w_query,
    w_key,
    w_value,
    w_out,
    b_query,
    b_value,
    b_out,
    gain_one,
    bias_one,
    w_image,
    b_image,
    c_query,
    c_key,
    c_value,
    c_out,
    cb_query,
    cb_value,
    cb_out,
    gain_two,
    bias_two,
    w_inner,
    b_inner,
    w_outer,
    b_outer,
    gain_three,
    bias_three,
    cotangent,
):
    count = lax.axis_size("mod") * lax.axis_size("dp")
    fold = count // LANES
    device = lax.axis_index("mod") * lax.axis_size("dp") + lax.axis_index("dp")
    place = device // fold
    core, chip = place % 2, place // 2
    first_core = core == 0

    def flip_device(block, mask):
        return lax.ppermute(block, AXES, [(i, i ^ mask) for i in range(count)])

    def flip_chip(block, mask):
        return flip_device(block, mask * 2 * fold)

    def flip_core(block):
        return flip_device(block, fold)

    def swap(block):
        return lax.ppermute(block, "mod", [(0, 1), (1, 0)])

    def gather_fold(shard):
        step = 1
        while step < fold:
            other = flip_device(shard, step)
            low = (device // step) % 2 == 0
            shard = jnp.concatenate(
                [jnp.where(low, shard, other), jnp.where(low, other, shard)], axis=0
            )
            step *= 2
        return shard

    def scatter_fold(total):
        step = fold // 2
        while step >= 1:
            low = (device // step) % 2 == 0
            half = total.shape[0] // 2
            kept = jnp.where(low, total[:half], total[half:])
            total = kept + flip_device(jnp.where(low, total[half:], total[:half]), step)
            step //= 2
        return total

    def split_rows(blocks, sizes):
        at, parts = 0, []
        for size in sizes:
            parts.append(blocks[..., at : at + size, :])
            at += size
        return parts

    def own_blocks(groups):
        kept, sent = pack_shards(core, [gather_fold(s) for g in groups for s in g])
        came = flip_core(sent)
        lows, highs = jnp.where(first_core, kept, came), jnp.where(first_core, came, kept)
        blocks, at = [], 0
        for g in groups:
            parts = []
            for shard in g:
                for _ in range(shard.shape[1] // D):
                    count = shard.shape[0] * fold
                    parts += [lows[at : at + count], highs[at : at + count]]
                    at += count
            blocks.append(jnp.concatenate(parts, axis=0))
        return blocks

    def spread(blocks, masks):
        return [flip_chip(blocks, m) for m in masks]

    def reduce_core(bufs):
        return [bufs[0], flip_core(bufs[1])]

    def add(*terms):
        return sum(t.astype(f32) for t in terms)

    def reduce_last(groups, terms):
        at, near = 0, []
        for pack, count in groups:
            kept, came = [t[:, at : at + count] for t in terms]
            far = flip_chip(add(kept[8:], came[8:]).astype(bf16), PACKS[pack][2][0])
            near += [kept[:8], came[:8], far]
            at += count
        return near

    def reduce_across(groups, near):
        blocks = []
        for i, (pack, _) in enumerate(groups):
            terms = near[3 * i : 3 * i + 3]
            across = flip_chip(add(*[t[4:] for t in terms]).astype(bf16), PACKS[pack][1][0])
            blocks.append(add(*[t[:4] for t in terms], across).astype(bf16))
        return jnp.concatenate(blocks, axis=1)

    def reduce_z(blocks):
        return add(blocks[0], *[flip_chip(blocks[j], ZS[j]) for j in range(1, 4)])

    def finish(total, sizes):
        mine, theirs = [], []
        for part in split_rows(total, sizes):
            half = part.shape[0] // 2
            mine.append(jnp.where(first_core, part[:half], part[half:]))
            theirs.append(jnp.where(first_core, part[half:], part[:half]))
        came = split_rows(flip_core(jnp.concatenate(theirs, axis=0)), [m.shape[0] for m in mine])
        result = []
        for part, other in zip(mine, came):
            joined = [jnp.where(first_core, part, other), jnp.where(first_core, other, part)]
            result.append(scatter_fold(jnp.concatenate(joined, axis=1)))
        return result

    def sum_near(total):
        step = 1
        while step <= fold:
            total = total + flip_device(total, step)
            step *= 2
        return total

    def hold(values, *after):
        count = len(values)
        return list(lax.optimization_barrier(tuple(values) + after)[:count])

    text_rows = swap(jnp.pad(text, ((0, 0), (0, TP - SEQ), (0, 0))).reshape(TR, D))
    cot_rows = jnp.pad(cotangent, ((0, 0), (0, TP - SEQ), (0, 0))).reshape(TR, D)
    item_lengths = swap(lengths)
    meta = jnp.concatenate([chip[None], core[None], item_lengths]).astype(jnp.int32)
    images = jnp.pad(patches, ((0, 0), (0, IP - NP), (0, 0))).reshape(IR, VW)
    params = join_params(
        *(b_query, b_value, b_out, gain_one, bias_one, b_image, cb_query),
        *(cb_value, cb_out, gain_two, bias_two, b_outer, gain_three, bias_three, b_inner),
    )
    w_outer = lax.all_gather(w_outer, AXES, axis=0, tiled=True)
    first, middle = own_blocks(
        [[w_query, w_key, w_value, c_query, c_out, w_image, c_key, c_value, w_out], [w_inner]]
    )
    first = jnp.stack([first] + spread(first, ZS[1:]))
    ma = jnp.stack([middle[:96], flip_chip(middle[:96], X)])
    mb = jnp.stack([middle[96:], flip_chip(middle[96:], Y)])
    ma = jnp.concatenate([ma, flip_chip(ma, Z0)])
    mb = jnp.concatenate([mb, flip_chip(mb, Z0)])
    a_4, b_4, ma, mb = hold(
        [first[:, :240], first[:, 240:], ma, mb], text_rows, item_lengths
    )
    a_8 = jnp.concatenate([a_4, flip_chip(a_4, X)])
    b_8 = jnp.concatenate([b_4, flip_chip(b_4, Y)])
    ma = jnp.concatenate([ma, flip_chip(ma, Z1)])
    a_8, b_8, ma, mb = hold([a_8, b_8, ma, mb])
    mb = jnp.concatenate([mb, flip_chip(mb, Z1)])
    a_far, b_far = flip_chip(a_8, Y), flip_chip(b_8, X)
    a_side, b_side = flip_core(a_8), flip_core(b_8)
    ma, mb, a_far, b_far, cot_rows = hold([ma, mb, a_far, b_far, cot_rows], a_side, b_side)
    cot_rows = swap(cot_rows)
    pack_a = [a_8, a_far, a_side, flip_core(a_far)]
    pack_b = [b_8, b_far, b_side, flip_core(b_far)]
    ma_far, mb_far = flip_chip(ma, Y), flip_chip(mb, X)
    qkv, img = ("a", pack_a, 0, 144), ("b", pack_b, 0, 160)
    mid = [("b", pack_b, 160, 48), ("a", pack_a, 144, 96)]
    qkv_sizes, img_sizes, mid_sizes = (48,) * 3, (64, 48, 48), (48,) * 3
    inner_sizes = (48,) * 4

    text_shape, image_shape = shape(TR, D), shape(IR, D)
    wide = shape(TR, D, dtype=f32)
    vec_shape = shape(8, D, dtype=f32)
    (q, k, v, attn, image_rows, ck, cv), _ = piece_kernel(
        first_front,
        "first_front",
        10,
        meta,
        [qkv, img],
        qkv_sizes + img_sizes,
        [],
        [text_rows, images, params],
        [text_shape] * 4 + [image_shape] * 3,
    )
    ma, mb, ma_far, mb_far, image_rows = hold([ma, mb, ma_far, mb_far, image_rows])
    inner = [
        ("ia", [ma, ma_far, flip_core(ma), flip_core(ma_far)], 0, 96),
        ("ib", [mb, mb_far, flip_core(mb), flip_core(mb_far)], 0, 96),
    ]
    (hidden, cq, cross, joint, sum_one, sum_two), _ = piece_kernel(
        mid_front,
        "mid_front",
        6,
        meta,
        mid,
        mid_sizes,
        [],
        [text_rows, attn, ck, cv, params],
        [text_shape] * 4 + [wide] * 2,
    )
    inner_groups, mid_groups = [("a", 96), ("b", 96)], [("b", 48), ("a", 96)]
    img_groups, qkv_groups = [("b", 160)], [("a", 144)]
    (mixed, grad_sum_two, vec_outer, vec_inner), (*inner_bufs, grad_w_outer) = piece_kernel(
        feed_forward,
        "feed_forward",
        17,
        meta,
        inner,
        inner_sizes,
        inner_groups,
        [joint, cot_rows, sum_two, params],
        [shape(ITEMS, SEQ, D, dtype=f32), wide, vec_shape, vec_shape],
        (
            [w_outer],
            [shape(FF, D)],
            [pltpu.VMEM((FF, D), bf16)] * 2
            + [pltpu.VMEM((TR, FF), bf16), pltpu.VMEM((TR, FF), f32), pltpu.VMEM((TR, FF), bf16)]
            + [pltpu.SemaphoreType.DMA((2,))],
        ),
    )
    grad_w_outer = lax.psum_scatter(grad_w_outer, AXES, scatter_dimension=0, tiled=True)
    inner_terms = reduce_core(inner_bufs)
    (grad_sum_one, grad_attn, dk, dv, vec_mid, _), mid_bufs = piece_kernel(
        mid_back,
        "mid_back",
        14,
        meta,
        mid,
        mid_sizes,
        mid_groups,
        [grad_sum_two, cross, hidden, attn, cq, ck, cv, sum_one, params],
        [wide, text_shape, image_shape, image_shape, vec_shape, text_shape],
    )
    dk, mixed, *inner_terms = hold([dk, mixed, *inner_terms])
    inner_near = reduce_last(inner_groups, inner_terms)
    mixed_out = swap(mixed)
    mid_terms = reduce_core(mid_bufs)
    (grad_patches, vec_image), img_bufs = piece_kernel(
        image_back,
        "image_back",
        12,
        meta,
        [img],
        img_sizes,
        img_groups,
        [images, image_rows, dk, dv],
        [shape(ITEMS, NP, VW, dtype=f32), vec_shape],
    )
    img_terms = reduce_core(img_bufs)
    grad_attn, mixed_out, *held = hold([grad_attn, mixed_out, vec_image, *mid_terms, *inner_near])
    vec_image, mid_terms, inner_near = held[0], held[1:3], held[3:]
    mid_near = reduce_last(mid_groups, mid_terms)
    inner_blocks = reduce_across(inner_groups, inner_near)
    (grad_text, vec_self, _, _, _), qkv_bufs = piece_kernel(
        self_back,
        "self_back",
        13,
        meta,
        [qkv],
        qkv_sizes,
        qkv_groups,
        [grad_attn, q, k, v, text_rows, grad_sum_one],
        [text_shape, vec_shape] + [text_shape] * 3,
    )
    qkv_terms = reduce_core(qkv_bufs)
    held = hold(
        [*img_terms, *qkv_terms, inner_blocks, grad_patches, grad_text, vec_self, *mid_near]
    )
    img_terms, qkv_terms, inner_blocks = held[:2], held[2:4], held[4]
    grad_patches, grad_text, vec_self = held[5:8]
    mid_near = held[8:]
    both_groups = img_groups + qkv_groups
    both_near = reduce_last(img_groups, img_terms) + reduce_last(qkv_groups, qkv_terms)
    mid_blocks = reduce_across(mid_groups, mid_near)
    inner_total = reduce_z(inner_blocks)
    vecs = sum_near(
        jnp.concatenate([vec_outer, vec_inner, vec_mid, vec_image, vec_self], axis=0)
    )
    mid_blocks, inner_total, vecs, *both_near = hold([mid_blocks, inner_total, vecs, *both_near])
    both_blocks = reduce_across(both_groups, both_near)
    mid_total = reduce_z(mid_blocks)
    vecs = vecs + flip_chip(vecs, Y)
    grad_text = swap(grad_text).reshape(ITEMS, TP, D)[:, :SEQ].astype(f32)
    both_blocks, mid_total, vecs = hold([both_blocks, mid_total, vecs])
    vecs = vecs + flip_chip(vecs, X)
    both_total = reduce_z(both_blocks)
    vecs = vecs + flip_chip(vecs, Z0)
    vecs = vecs + flip_chip(vecs, Z1)
    img_total, qkv_total = both_total[:160], both_total[160:]
    grad_w_inner = jnp.concatenate(finish(inner_total, inner_sizes), axis=1)
    grad_w_out, grad_c_query, grad_c_out = finish(mid_total, mid_sizes)
    grad_w_image, grad_c_key, grad_c_value = finish(img_total, img_sizes)
    grad_w_query, grad_w_key, grad_w_value = finish(qkv_total, qkv_sizes)
    grad_b_inner = vecs[4:8].reshape(FF)
    return (
        mixed_out,
        grad_text,
        grad_patches,
        grad_w_query,
        grad_w_key,
        grad_w_value,
        grad_w_out,
        vecs[32],
        vecs[33],
        vecs[20],
        vecs[18],
        vecs[19],
        grad_w_image,
        vecs[25],
        grad_c_query,
        grad_c_key,
        grad_c_value,
        grad_c_out,
        vecs[17],
        vecs[24],
        vecs[16],
        vecs[8],
        vecs[9],
        grad_w_inner,
        grad_b_inner,
        grad_w_outer.astype(f32),
        vecs[2],
        vecs[0],
        vecs[1],
    )


def solution(mesh):
    items = P(AXES, None, None)
    shard, whole = P(AXES, None), P()
    in_specs = (
        (items, P(AXES), items)
        + (shard,) * 4
        + (whole,) * 5
        + (shard, whole)
        + (shard,) * 4
        + (whole,) * 5
        + (shard, whole, shard)
        + (whole,) * 3
        + (items,)
    )
    out_specs = (
        (items,) * 3
        + (shard,) * 4
        + (whole,) * 5
        + (shard, whole)
        + (shard,) * 4
        + (whole,) * 5
        + (shard, whole, shard)
        + (whole,) * 3
    )
    return jax.shard_map(local, mesh=mesh, in_specs=in_specs, out_specs=out_specs, check_vma=False)
```

```python
import jax
import jax.numpy as jnp
from jax import lax
from jax.experimental import pallas as pl
from jax.experimental.pallas import tpu as pltpu
from jax.sharding import PartitionSpec as P

D = 768
HD = 64
GROUP = 256
NGROUP = 3
PER = 4
VW = 1024
NP = 145
SEQ = 40
ITEMS = 4
TP = 48
IP = 160
TR = ITEMS * TP
IR = ITEMS * IP
FF = 3072
HALF = D // 2
CHIPS = 16
LANES = CHIPS * 2
SCALE = HD**-0.5
neg_large = -1000000000.0
ln_eps = 1e-06
bf16 = jnp.bfloat16
f32 = jnp.float32
AXES = ("mod", "dp")
MICRO = 1.1e9

Y, Z0, Z1, X = 1, 2, 4, 8
ZS = (0, Z0, Z1, Z0 | Z1)


def held_by(*masks):
    held = [0]
    for group in masks:
        held += [h ^ m for m in group for h in held]
    return held


PACKS = {
    "a": (ZS[1:], (X,), (Y,)),
    "b": (ZS[1:], (Y,), (X,)),
    "ia": ((X,), ZS[1:], (Y,)),
    "ib": ((Y,), ZS[1:], (X,)),
}


def mm(a, b):
    return jnp.dot(a, b, preferred_element_type=f32)


def mm_t(a, b):
    return lax.dot_general(a, b, (((1,), (1,)), ((), ())), preferred_element_type=f32)


def mm_w(a, b):
    return lax.dot_general(a, b, (((0,), (0,)), ((), ())), preferred_element_type=f32)


def rowsum(a):
    return jnp.sum(a.astype(f32), axis=0, keepdims=True)


def ln_parts(v):
    centered = v - jnp.mean(v, axis=-1, keepdims=True)
    spread = jnp.mean(centered * centered, axis=-1, keepdims=True)
    scale = lax.rsqrt(spread + ln_eps)
    return centered * scale, scale


def ln_back(grad, normed, scale, gain):
    a = grad * gain
    inner = a - jnp.mean(a, axis=-1, keepdims=True)
    return scale * (inner - normed * jnp.mean(a * normed, axis=-1, keepdims=True))


def head_masks():
    head = lax.broadcasted_iota(jnp.int32, (1, GROUP), 1) // HD
    return [jnp.where(head == h, 1.0, 0.0) for h in range(PER)]


def expand(rows, masks):
    return jnp.concatenate([rows * m.astype(bf16) for m in masks], axis=0)


def collapse(full, masks):
    total = full[0:TP] * masks[0]
    for h in range(1, PER):
        total = total + full[h * TP : (h + 1) * TP] * masks[h]
    return total


def softmax_rows(scores):
    e = jnp.exp(scores - jnp.max(scores, axis=-1, keepdims=True))
    return e / jnp.sum(e, axis=-1, keepdims=True)


def attend_forward(q_ref, k_ref, v_ref, o_ref, key_rows, length_of):
    masks = head_masks()
    column = lax.broadcasted_iota(jnp.int32, (1, key_rows), 1)

    def item(i, carry):
        rows = pl.ds(pl.multiple_of(i * TP, 16), TP)
        keys = pl.ds(pl.multiple_of(i * key_rows, 16), key_rows)
        bias = jnp.where(column < length_of(i), 0.0, neg_large)
        for g in range(NGROUP):
            lanes = slice(g * GROUP, (g + 1) * GROUP)
            q = expand(q_ref[rows, lanes], masks)
            probs = softmax_rows(mm_t(q, k_ref[keys, lanes]) * SCALE + bias)
            out = mm(probs.astype(bf16), v_ref[keys, lanes])
            o_ref[rows, lanes] = collapse(out, masks).astype(bf16)
        return carry

    lax.fori_loop(0, ITEMS, item, 0, unroll=True)


def attend_backward(go_ref, q_ref, k_ref, v_ref, dq_ref, dk_ref, dv_ref, key_rows, length_of):
    masks = head_masks()
    column = lax.broadcasted_iota(jnp.int32, (1, key_rows), 1)

    def item(i, carry):
        rows = pl.ds(pl.multiple_of(i * TP, 16), TP)
        keys = pl.ds(pl.multiple_of(i * key_rows, 16), key_rows)
        bias = jnp.where(column < length_of(i), 0.0, neg_large)
        for g in range(NGROUP):
            lanes = slice(g * GROUP, (g + 1) * GROUP)
            q = expand(q_ref[rows, lanes], masks)
            k = k_ref[keys, lanes]
            probs = softmax_rows(mm_t(q, k) * SCALE + bias)
            go = expand(go_ref[rows, lanes], masks)
            dp = mm_t(go, v_ref[keys, lanes])
            ds = (probs * (dp - jnp.sum(probs * dp, axis=-1, keepdims=True))).astype(bf16)
            dq_ref[rows, lanes] = (collapse(mm(ds, k), masks) * SCALE).astype(bf16)
            dk_ref[keys, lanes] = (mm_w(ds, q) * SCALE).astype(bf16)
            dv_ref[keys, lanes] = mm_w(probs.astype(bf16), go).astype(bf16)
        return carry

    lax.fori_loop(0, ITEMS, item, 0, unroll=True)


def whole_block(x):
    zeros = (0,) * len(x.shape)
    return pl.BlockSpec(x.shape, lambda i: zeros, pipeline_mode=pl.Buffered(1))


def piece_kernel(body, name, micros, meta, weights, sizes, grads, ins, outs, far=()):
    rows = sum(sizes)
    far_in, far_out, far_scratch = far or ((), (), ())
    n_in, n_out = len(ins), len(outs)
    hbm_in = [buf for _, bufs, _, _ in weights for buf in bufs]
    n_buf = len(hbm_in)
    grad_shapes = [shape(CHIPS, rows, HALF)] * 2 if grads else []
    n_grad = len(grad_shapes)

    def kernel(*refs):
        meta_ref, refs = refs[0], refs[1:]
        in_refs, refs = refs[:n_in], refs[n_in:]
        buf_refs, refs = refs[:n_buf], refs[n_buf:]
        far_refs, refs = refs[: len(far_in)], refs[len(far_in) :]
        out_refs, refs = refs[:n_out], refs[n_out:]
        grad_refs, refs = refs[:n_grad], refs[n_grad:]
        far_refs, refs = far_refs + refs[: len(far_out)], refs[len(far_out) :]
        far_refs, refs = far_refs + refs[: len(far_scratch)], refs[len(far_scratch) :]
        if weights:
            (w_ref, load_sem), refs = refs[:2], refs[2:]
        if grads:
            g_ref, store_sem = refs
        chip, core = meta_ref[0], meta_ref[1]
        columns = [
            pl.ds(pl.multiple_of(core * HALF, 128), HALF),
            pl.ds(pl.multiple_of((1 - core) * HALF, 128), HALF),
        ]

        def load_copies():
            made, at = [], 0
            for i, (pack, _, first, count) in enumerate(weights):
                for side in range(2):
                    for j, mask in enumerate(held_by(*PACKS[pack])):
                        source = buf_refs[4 * i + side * 2 + j // 8]
                        outside = source.at[j % 8, first : first + count, :]
                        inside = w_ref.at[chip ^ mask, at : at + count, columns[side]]
                        copy = pltpu.make_async_copy(outside, inside, load_sem.at[len(made)])
                        made.append(copy)
                at += count
            return made

        def store_copies(k):
            low, pack, at = sum(sizes[:k]), None, 0
            for name_of, count in grads:
                if at <= low < at + count:
                    pack = name_of
                at += count
            rows_of, made = slice(low, low + sizes[k]), []
            for side in range(2):
                for j, mask in enumerate(held_by(*PACKS[pack])):
                    inside = g_ref.at[chip ^ mask, rows_of, columns[side]]
                    sem = store_sem.at[k * LANES + len(made)]
                    outside = grad_refs[side].at[j, rows_of, :]
                    made.append(pltpu.make_async_copy(inside, outside, sem))
            return made

        loads = load_copies() if weights else []
        stores = []
        for copy in loads:
            copy.start()

        def ready(group):
            for copy in loads[group * LANES : (group + 1) * LANES]:
                copy.wait()

        def weight(k):
            low = sum(sizes[:k])
            return w_ref[:, low : low + sizes[k], :].reshape(CHIPS * sizes[k], D)

        def put(k, value):
            low = sum(sizes[:k])
            g_ref[:, low : low + sizes[k], :] = value.astype(bf16).reshape(CHIPS, sizes[k], D)
            for copy in store_copies(k):
                copy.start()
                stores.append(copy)

        body(meta_ref, ready, weight, put, in_refs, out_refs + far_refs)
        for copy in stores:
            copy.wait()

    hbm = pl.BlockSpec(memory_space=pl.ANY)
    scratch = list(far_scratch)
    if weights:
        scratch += [
            pltpu.VMEM((CHIPS, rows, D), bf16),
            pltpu.SemaphoreType.DMA((LANES * len(weights),)),
        ]
    if grads:
        scratch += [
            pltpu.VMEM((CHIPS, rows, D), bf16),
            pltpu.SemaphoreType.DMA((LANES * len(sizes),)),
        ]
    made = pl.pallas_call(
        kernel,
        out_shape=list(outs) + grad_shapes + list(far_out),
        grid=(1,),
        in_specs=[pl.BlockSpec(memory_space=pltpu.SMEM)]
        + [whole_block(x) for x in ins]
        + [hbm] * (n_buf + len(far_in)),
        out_specs=[whole_block(x) for x in outs] + [hbm] * (n_grad + len(far_out)),
        scratch_shapes=scratch,
        compiler_params=pltpu.CompilerParams(vmem_limit_bytes=(60 if far_in else 50) * 1024 * 1024),
        cost_estimate=pl.CostEstimate(
            flops=int(micros * MICRO), bytes_accessed=0, transcendentals=0
        ),
        name=name,
    )(meta, *ins, *hbm_in, *far_in)
    return made[:n_out], made[n_out:]


PARAMS = (
    "b_query",
    "b_value",
    "b_out",
    "gain_one",
    "bias_one",
    "b_image",
    "cb_query",
    "cb_value",
    "cb_out",
    "gain_two",
    "bias_two",
    "b_outer",
    "gain_three",
    "bias_three",
)
B_INNER = 16


def param(ref, name):
    at = PARAMS.index(name)
    return ref[at : at + 1]


def join_params(*vectors):
    def kernel(*refs):
        out = refs[-1]
        for i, ref in enumerate(refs[:-2]):
            out[i : i + 1] = ref[...].reshape(1, D)
        out[len(PARAMS) : B_INNER] = jnp.zeros((B_INNER - len(PARAMS), D), f32)
        inner = refs[-2][...].reshape(1, FF)
        for k in range(4):
            out[B_INNER + k : B_INNER + k + 1] = inner[:, k * D : (k + 1) * D]
        out[B_INNER + 4 :] = jnp.zeros((4, D), f32)

    vmem = pl.BlockSpec(memory_space=pltpu.VMEM)
    return pl.pallas_call(
        kernel,
        out_shape=shape(24, D, dtype=f32),
        in_specs=[vmem] * len(vectors),
        out_specs=vmem,
        name="join_params",
    )(*vectors)


def pack_shards(core, shards):
    rows = sum(s.shape[0] * (s.shape[1] // D) for s in shards)

    def kernel(core_ref, *refs):
        parts = []
        for ref in refs[:-2]:
            full = ref[...].astype(f32)
            parts += [full[:, k * D : (k + 1) * D] for k in range(full.shape[1] // D)]
        full = jnp.concatenate(parts, axis=0)
        second = core_ref[0] > 0
        low, high = full[:, :HALF], full[:, HALF:]
        refs[-2][...] = jnp.where(second, high, low).astype(bf16)
        refs[-1][...] = jnp.where(second, low, high).astype(bf16)

    vmem = pl.BlockSpec(memory_space=pltpu.VMEM)
    return pl.pallas_call(
        kernel,
        out_shape=[shape(rows, HALF)] * 2,
        in_specs=[pl.BlockSpec(memory_space=pltpu.SMEM)] + [vmem] * len(shards),
        out_specs=[vmem] * 2,
        name="pack_shards",
    )(core[None].astype(jnp.int32), *shards)


def small_call(kernel, name, core, ins, outs):
    vmem = pl.BlockSpec(memory_space=pltpu.VMEM)
    return pl.pallas_call(
        kernel,
        out_shape=outs,
        in_specs=[pl.BlockSpec(memory_space=pltpu.SMEM)] + [vmem] * len(ins),
        out_specs=[vmem] * len(outs),
        name=name,
    )(core[None].astype(jnp.int32), *ins)


def split_cores(core, pieces):
    rows = sum(sum(sizes) for _, sizes in pieces) // 2

    def kernel(core_ref, *refs):
        second = core_ref[0] > 0
        out = 0
        for i, (_, sizes) in enumerate(pieces):
            total = refs[4 * i][...].astype(f32)
            for ref in refs[4 * i + 1 : 4 * i + 4]:
                total = total + ref[...].astype(f32)
            at = 0
            for size in sizes:
                half = size // 2
                low, high = total[at : at + half], total[at + half : at + size]
                refs[-2][out : out + half] = jnp.where(second, high, low)
                refs[-1][out : out + half] = jnp.where(second, low, high)
                at, out = at + size, out + half

    ins = [term for terms, _ in pieces for term in terms]
    return small_call(kernel, "split_cores", core, ins, [shape(rows, HALF, dtype=f32)] * 2)


def join_halves(core, mine, came, counts):
    def kernel(core_ref, mine_ref, came_ref, *outs):
        second, at = core_ref[0] > 0, 0
        for out, (rows, wide) in zip(outs, counts):
            for k in range(wide):
                a, b = mine_ref[at : at + rows], came_ref[at : at + rows]
                out[:, k * D : k * D + HALF] = jnp.where(second, b, a)
                out[:, k * D + HALF : (k + 1) * D] = jnp.where(second, a, b)
                at += rows

    outs = [shape(rows, wide * D, dtype=f32) for rows, wide in counts]
    return small_call(kernel, "join_halves", core, [mine, came], outs)


def shape(*dims, dtype=bf16):
    return jax.ShapeDtypeStruct(dims, dtype)


def first_front(meta, ready, weight, put, ins, outs):
    text, images, params = ins
    q, k, v, attn, image_rows, ck, cv = outs
    ready(0)
    rows = text[:TR]
    q[...] = (mm(rows, weight(0)) + param(params, "b_query")).astype(bf16)
    k[...] = mm(rows, weight(1)).astype(bf16)
    v[...] = (mm(rows, weight(2)) + param(params, "b_value")).astype(bf16)
    attend_forward(q, k, v, attn, TP, lambda i: meta[2 + i])
    ready(1)
    image_rows[...] = (mm(images[...], weight(3)) + param(params, "b_image")).astype(bf16)
    ck[...] = mm(image_rows[...], weight(4)).astype(bf16)
    cv[...] = (mm(image_rows[...], weight(5)) + param(params, "cb_value")).astype(bf16)


def mid_front(meta, ready, weight, put, ins, outs):
    text, attn, ck, cv, params = ins
    hidden, cq, cross, joint, sum_one, sum_two = outs
    ready(0)
    ready(1)
    sum_one[...] = text[:TR].astype(f32) + (mm(attn[...], weight(0)) + param(params, "b_out"))
    normed, _ = ln_parts(sum_one[...])
    hidden[...] = (normed * param(params, "gain_one") + param(params, "bias_one")).astype(bf16)
    cq[...] = (mm(hidden[...], weight(1)) + param(params, "cb_query")).astype(bf16)
    attend_forward(cq, ck, cv, cross, IP, lambda i: NP)
    sum_two[...] = hidden[...].astype(f32) + (mm(cross[...], weight(2)) + param(params, "cb_out"))
    normed, _ = ln_parts(sum_two[...])
    joint[...] = (normed * param(params, "gain_two") + param(params, "bias_two")).astype(bf16)


def feed_forward(meta, ready, weight, put, ins, outs):
    joint, cot, sum_two, params = ins
    mixed, grad_sum_two, vec_three, vec_two = outs[:4]
    outer_hbm, grad_outer_hbm, outer_w, grad_outer_w, active, slope, grad_inner, sem = outs[4:]
    load = pltpu.make_async_copy(outer_hbm, outer_w, sem.at[0])
    load.start()
    ready(0)
    ready(1)
    for k in range(4):
        lanes = slice(k * D, (k + 1) * D)
        pre = mm(joint[...], weight(k)) + params[B_INNER + k : B_INNER + k + 1]
        cdf = 0.5 * (1.0 + lax.erf(pre * 0.5**0.5))
        active[:, lanes] = (pre * cdf).astype(bf16)
        slope[:, lanes] = cdf + pre * (jnp.exp(-0.5 * pre * pre) * 0.3989422804014327)
    load.wait()
    outer = mm(active[...], outer_w[...]) + param(params, "b_outer")
    normed, scale = ln_parts(joint[...].astype(f32) + outer)
    gain = param(params, "gain_three")
    result = normed * gain + param(params, "bias_three")
    row = lax.broadcasted_iota(jnp.int32, (TP, 1), 0)
    keep = [jnp.where(row < meta[2 + i], 1.0, 0.0) for i in range(ITEMS)]
    for i in range(ITEMS):
        mixed[i] = (result[i * TP : (i + 1) * TP] * keep[i])[:SEQ]
    grad = cot[...].astype(f32) * jnp.concatenate(keep, axis=0)
    grad_sum = ln_back(grad, normed, scale, gain)
    grad_outer = grad_sum.astype(bf16)
    vec_three[0:1] = rowsum(grad * normed)
    vec_three[1:2] = rowsum(grad)
    vec_three[2:3] = rowsum(grad_outer)
    vec_three[3:4] = jnp.zeros((1, D), f32)
    grad_outer_w[...] = mm_w(active[...], grad_outer).astype(bf16)
    store = pltpu.make_async_copy(grad_outer_w, grad_outer_hbm, sem.at[1])
    store.start()
    for k in range(4):
        lanes = slice(k * D, (k + 1) * D)
        part = (slope[:, lanes] * mm_t(grad_outer, outer_w[lanes, :])).astype(bf16)
        grad_inner[:, lanes] = part
        vec_three[4 + k : 5 + k] = rowsum(part)
        put(k, mm_w(joint[...], part))
    grad = grad_sum
    for k in range(4):
        grad = grad + mm_t(grad_inner[:, k * D : (k + 1) * D], weight(k))
    normed, scale = ln_parts(sum_two[...])
    grad_sum_two[...] = ln_back(grad, normed, scale, param(params, "gain_two"))
    vec_two[...] = jnp.concatenate(
        [rowsum(grad * normed), rowsum(grad), jnp.zeros((6, D), f32)], axis=0
    )
    store.wait()


def mid_back(meta, ready, weight, put, ins, outs):
    grad_sum_two, cross, hidden, attn, cq, ck, cv, sum_one, params = ins
    grad_sum_one, grad_attn, dk, dv, vec, dq, grad_cross = outs
    gain = param(params, "gain_one")
    grad_cross_branch = grad_sum_two[...].astype(bf16)
    ready(0)
    ready(1)
    grad_cross[...] = mm_t(grad_cross_branch, weight(2)).astype(bf16)
    attend_backward(grad_cross, cq, ck, cv, dq, dk, dv, IP, lambda i: NP)
    put(2, mm_w(cross[...], grad_cross_branch))
    put(1, mm_w(hidden[...], dq[...]))
    grad = grad_sum_two[...] + mm_t(dq[...], weight(1))
    normed, scale = ln_parts(sum_one[...])
    grad_sum_one[...] = ln_back(grad, normed, scale, gain)
    grad_branch = grad_sum_one[...].astype(bf16)
    put(0, mm_w(attn[...], grad_branch))
    grad_attn[...] = mm_t(grad_branch, weight(0)).astype(bf16)
    vec[...] = jnp.concatenate(
        [
            rowsum(grad_cross_branch),
            rowsum(dq[...]),
            rowsum(grad * normed),
            rowsum(grad),
            rowsum(grad_branch),
            jnp.zeros((3, D), f32),
        ],
        axis=0,
    )


def image_back(meta, ready, weight, put, ins, outs):
    images, image_rows, dk, dv = ins
    grad_patches, vec = outs
    put(1, mm_w(image_rows[...], dk[...]))
    put(2, mm_w(image_rows[...], dv[...]))
    ready(0)
    grad_image = (mm_t(dk[...], weight(1)) + mm_t(dv[...], weight(2))).astype(bf16)
    put(0, mm_w(images[...], grad_image))
    for i in range(ITEMS):
        grad_patches[i] = mm_t(grad_image[i * IP : (i + 1) * IP], weight(0))[:NP]
    vec[...] = jnp.concatenate([rowsum(dv[...]), rowsum(grad_image), jnp.zeros((6, D), f32)], axis=0)


def self_back(meta, ready, weight, put, ins, outs):
    grad_attn, q, k, v, text, grad_sum_one = ins
    grad_text, vec, dq, dk, dv = outs
    attend_backward(grad_attn, q, k, v, dq, dk, dv, TP, lambda i: meta[2 + i])
    put(0, mm_w(text[:TR], dq[...]))
    put(1, mm_w(text[:TR], dk[...]))
    put(2, mm_w(text[:TR], dv[...]))
    ready(0)
    total = grad_sum_one[...] + mm_t(dq[...], weight(0))
    total = total + mm_t(dk[...], weight(1))
    grad_text[...] = (total + mm_t(dv[...], weight(2))).astype(bf16)
    vec[...] = jnp.concatenate([rowsum(dq[...]), rowsum(dv[...]), jnp.zeros((6, D), f32)], axis=0)


def local(
    text,
    lengths,
    patches,
    w_query,
    w_key,
    w_value,
    w_out,
    b_query,
    b_value,
    b_out,
    gain_one,
    bias_one,
    w_image,
    b_image,
    c_query,
    c_key,
    c_value,
    c_out,
    cb_query,
    cb_value,
    cb_out,
    gain_two,
    bias_two,
    w_inner,
    b_inner,
    w_outer,
    b_outer,
    gain_three,
    bias_three,
    cotangent,
):
    count = lax.axis_size("mod") * lax.axis_size("dp")
    fold = count // LANES
    device = lax.axis_index("mod") * lax.axis_size("dp") + lax.axis_index("dp")
    place = device // fold
    core, chip = place % 2, place // 2
    first_core = core == 0

    def flip_device(block, mask):
        return lax.ppermute(block, AXES, [(i, i ^ mask) for i in range(count)])

    def flip_chip(block, mask):
        return flip_device(block, mask * 2 * fold)

    def flip_core(block):
        return flip_device(block, fold)

    def swap(block):
        return lax.ppermute(block, "mod", [(0, 1), (1, 0)])

    def gather_fold(shard):
        step = 1
        while step < fold:
            other = flip_device(shard, step)
            low = (device // step) % 2 == 0
            shard = jnp.concatenate(
                [jnp.where(low, shard, other), jnp.where(low, other, shard)], axis=0
            )
            step *= 2
        return shard

    def scatter_fold(total):
        step = fold // 2
        while step >= 1:
            low = (device // step) % 2 == 0
            half = total.shape[0] // 2
            kept = jnp.where(low, total[:half], total[half:])
            total = kept + flip_device(jnp.where(low, total[half:], total[:half]), step)
            step //= 2
        return total

    def split_rows(blocks, sizes):
        at, parts = 0, []
        for size in sizes:
            parts.append(blocks[..., at : at + size, :])
            at += size
        return parts

    def own_blocks(groups):
        kept, sent = pack_shards(core, [gather_fold(s) for g in groups for s in g])
        came = flip_core(sent)
        lows, highs = jnp.where(first_core, kept, came), jnp.where(first_core, came, kept)
        blocks, at = [], 0
        for g in groups:
            parts = []
            for shard in g:
                for _ in range(shard.shape[1] // D):
                    count = shard.shape[0] * fold
                    parts += [lows[at : at + count], highs[at : at + count]]
                    at += count
            blocks.append(jnp.concatenate(parts, axis=0))
        return blocks

    def spread(blocks, masks):
        return [flip_chip(blocks, m) for m in masks]

    def reduce_core(bufs):
        return [bufs[0], flip_core(bufs[1])]

    def add(*terms):
        return sum(t.astype(f32) for t in terms)

    def reduce_last(groups, terms):
        at, near = 0, []
        for pack, count in groups:
            kept, came = [t[:, at : at + count] for t in terms]
            far = flip_chip(add(kept[8:], came[8:]).astype(bf16), PACKS[pack][2][0])
            near += [kept[:8], came[:8], far]
            at += count
        return near

    def reduce_across(groups, near):
        blocks = []
        for i, (pack, _) in enumerate(groups):
            terms = near[3 * i : 3 * i + 3]
            across = flip_chip(add(*[t[4:] for t in terms]).astype(bf16), PACKS[pack][1][0])
            blocks.append(add(*[t[:4] for t in terms], across).astype(bf16))
        return jnp.concatenate(blocks, axis=1)

    def reduce_across_all(groups, near):
        blocks = []
        for pack in ("a", "b"):
            terms = [near[3 * i : 3 * i + 3] for i, g in enumerate(groups) if g[0] == pack]
            sent = [add(*[t[4:] for t in ts]).astype(bf16) for ts in terms]
            across = flip_chip(jnp.concatenate(sent, axis=1), PACKS[pack][1][0])
            kept = jnp.concatenate([add(*[t[:4] for t in ts]) for ts in terms], axis=1)
            blocks.append(add(kept, across).astype(bf16))
        return jnp.concatenate(blocks, axis=1)

    def reduce_z(blocks):
        return [blocks[0]] + [flip_chip(blocks[j], ZS[j]) for j in range(1, 4)]

    def finish(pieces, counts):
        mine, theirs = split_cores(core, pieces)
        return [scatter_fold(w) for w in join_halves(core, mine, flip_core(theirs), counts)]

    def sum_near(total):
        step = 1
        while step <= fold:
            total = total + flip_device(total, step)
            step *= 2
        return total

    def hold(values, *after):
        count = len(values)
        return list(lax.optimization_barrier(tuple(values) + after)[:count])

    text_rows = jnp.pad(text, ((0, 0), (0, TP - SEQ), (0, 0))).reshape(TR, D)
    lengths_row = jnp.pad(lengths.astype(bf16)[None], ((0, 15), (0, D - ITEMS)))
    text_rows = swap(jnp.concatenate([text_rows, lengths_row], axis=0))
    item_lengths = text_rows[TR, :ITEMS]
    cot_rows = jnp.pad(cotangent, ((0, 0), (0, TP - SEQ), (0, 0))).reshape(TR, D)
    meta = jnp.concatenate([chip[None], core[None], item_lengths.astype(jnp.int32)]).astype(jnp.int32)
    images = jnp.pad(patches, ((0, 0), (0, IP - NP), (0, 0))).reshape(IR, VW)
    params = join_params(
        *(b_query, b_value, b_out, gain_one, bias_one, b_image, cb_query),
        *(cb_value, cb_out, gain_two, bias_two, b_outer, gain_three, bias_three, b_inner),
    )
    w_outer = lax.all_gather(w_outer, AXES, axis=0, tiled=True)
    first, middle = own_blocks(
        [[w_query, w_key, w_value, c_query, c_out, w_image, c_key, c_value, w_out], [w_inner]]
    )
    first = jnp.stack([first] + spread(first, ZS[1:]))
    ma = jnp.stack([middle[:96], flip_chip(middle[:96], X)])
    mb = jnp.stack([middle[96:], flip_chip(middle[96:], Y)])
    middle = jnp.concatenate([ma, mb], axis=1)
    middle = jnp.concatenate([middle, flip_chip(middle, Z0)])
    a_4, b_4, ma, mb = hold(
        [first[:, :240], first[:, 240:], middle[:, :96], middle[:, 96:]], text_rows
    )
    a_8 = jnp.concatenate([a_4, flip_chip(a_4, X)])
    b_8 = jnp.concatenate([b_4, flip_chip(b_4, Y)])
    ma = jnp.concatenate([ma, flip_chip(ma, Z1)])
    a_8, b_8, ma, mb = hold([a_8, b_8, ma, mb])
    mb = jnp.concatenate([mb, flip_chip(mb, Z1)])
    a_far, b_far = flip_chip(a_8, Y), flip_chip(b_8, X)
    a_side, b_side = flip_core(a_8), flip_core(b_8)
    ma, mb, a_far, b_far, cot_rows = hold([ma, mb, a_far, b_far, cot_rows], a_side, b_side)
    cot_rows = swap(cot_rows)
    pack_a = [a_8, a_far, a_side, flip_core(a_far)]
    pack_b = [b_8, b_far, b_side, flip_core(b_far)]
    ma_far, mb_far = flip_chip(ma, Y), flip_chip(mb, X)
    qkv, img = ("a", pack_a, 0, 144), ("b", pack_b, 0, 160)
    mid = [("b", pack_b, 160, 48), ("a", pack_a, 144, 96)]
    qkv_sizes, img_sizes, mid_sizes = (48,) * 3, (64, 48, 48), (48,) * 3
    inner_sizes = (48,) * 4

    text_shape, image_shape = shape(TR, D), shape(IR, D)
    wide = shape(TR, D, dtype=f32)
    vec_shape = shape(8, D, dtype=f32)
    (q, k, v, attn, image_rows, ck, cv), _ = piece_kernel(
        first_front,
        "first_front",
        10,
        meta,
        [qkv, img],
        qkv_sizes + img_sizes,
        [],
        [text_rows, images, params],
        [text_shape] * 4 + [image_shape] * 3,
    )
    ma, mb, ma_far, mb_far, image_rows = hold([ma, mb, ma_far, mb_far, image_rows])
    inner = [
        ("ia", [ma, ma_far, flip_core(ma), flip_core(ma_far)], 0, 96),
        ("ib", [mb, mb_far, flip_core(mb), flip_core(mb_far)], 0, 96),
    ]
    (hidden, cq, cross, joint, sum_one, sum_two), _ = piece_kernel(
        mid_front,
        "mid_front",
        6,
        meta,
        mid,
        mid_sizes,
        [],
        [text_rows, attn, ck, cv, params],
        [text_shape] * 4 + [wide] * 2,
    )
    inner_groups, mid_groups = [("a", 96), ("b", 96)], [("b", 96), ("a", 48)]
    img_groups, qkv_groups = [("b", 160)], [("a", 144)]
    (mixed, grad_sum_two, vec_outer, vec_inner), (*inner_bufs, grad_w_outer) = piece_kernel(
        feed_forward,
        "feed_forward",
        17,
        meta,
        inner,
        inner_sizes,
        inner_groups,
        [joint, cot_rows, sum_two, params],
        [shape(ITEMS, SEQ, D, dtype=f32), wide, vec_shape, vec_shape],
        (
            [w_outer],
            [shape(FF, D)],
            [pltpu.VMEM((FF, D), bf16)] * 2
            + [pltpu.VMEM((TR, FF), bf16), pltpu.VMEM((TR, FF), f32), pltpu.VMEM((TR, FF), bf16)]
            + [pltpu.SemaphoreType.DMA((2,))],
        ),
    )
    grad_w_outer = lax.psum_scatter(grad_w_outer, AXES, scatter_dimension=0, tiled=True)
    inner_terms = reduce_core(inner_bufs)
    (grad_sum_one, grad_attn, dk, dv, vec_mid), mid_bufs = piece_kernel(
        mid_back,
        "mid_back",
        14,
        meta,
        mid,
        mid_sizes,
        mid_groups,
        [grad_sum_two, cross, hidden, attn, cq, ck, cv, sum_one, params],
        [wide, text_shape, image_shape, image_shape, vec_shape],
        ((), (), [pltpu.VMEM((TR, D), bf16)] * 2),
    )
    dk, mixed_out, *inner_terms = hold([dk, swap(mixed), *inner_terms])
    inner_near = reduce_last(inner_groups, inner_terms)
    mid_terms = reduce_core(mid_bufs)
    (grad_patches, vec_image), img_bufs = piece_kernel(
        image_back,
        "image_back",
        12,
        meta,
        [img],
        img_sizes,
        img_groups,
        [images, image_rows, dk, dv],
        [shape(ITEMS, NP, VW, dtype=f32), vec_shape],
    )
    img_terms = reduce_core(img_bufs)
    grad_attn, *held = hold([grad_attn, vec_image, *mid_terms, *inner_near])
    vec_image, mid_terms, inner_near = held[0], held[1:3], held[3:]
    mid_near = reduce_last(mid_groups, mid_terms)
    inner_blocks = reduce_across(inner_groups, inner_near)
    (grad_text, vec_self), qkv_bufs = piece_kernel(
        self_back,
        "self_back",
        13,
        meta,
        [qkv],
        qkv_sizes,
        qkv_groups,
        [grad_attn, q, k, v, text_rows, grad_sum_one],
        [text_shape, vec_shape],
        ((), (), [pltpu.VMEM((TR, D), bf16)] * 3),
    )
    inner_blocks, grad_patches, *held = hold(
        [inner_blocks, grad_patches, vec_self, *qkv_bufs, *img_terms, *mid_near]
    )
    vec_self, qkv_bufs, img_terms, mid_near = held[0], held[1:3], held[3:5], held[5:]
    both_near = reduce_last(img_groups, img_terms) + reduce_last(
        qkv_groups, reduce_core(qkv_bufs)
    )
    rows = [vec_outer[:3], vec_outer[4:8], vec_inner[:2], vec_mid[:5], vec_image[:2], vec_self[:2]]
    vecs = sum_near(jnp.concatenate(rows + [jnp.zeros((6, D), f32)], axis=0))
    vecs = sum([flip_chip(vecs, z) for z in ZS[1:]], vecs)
    held = hold([inner_blocks, vecs, *mid_near, *both_near])
    inner_blocks, vecs, mid_near, both_near = held[0], held[1], held[2:8], held[8:]
    blocks = reduce_across_all(mid_groups + img_groups + qkv_groups, mid_near + both_near)
    inner_terms = reduce_z(inner_blocks)
    blocks, vecs, grad_text, *inner_terms = hold(
        [blocks, vecs, grad_text, *inner_terms]
    )
    terms = reduce_z(blocks)
    vecs = sum([flip_chip(vecs, m) for m in (X, Y, X | Y)], vecs)
    grad_text = swap(grad_text).reshape(ITEMS, TP, D)[:, :SEQ].astype(f32)
    vecs, *inner_terms = hold([vecs, *inner_terms])
    (grad_w_inner,) = finish([(inner_terms, inner_sizes)], [(24, 4)])
    (
        grad_c_out,
        grad_w_query,
        grad_w_key,
        grad_w_value,
        grad_w_out,
        grad_c_query,
        grad_w_image,
        grad_c_key,
        grad_c_value,
    ) = finish([(terms, (48,) * 6 + img_sizes)], [(24, 1)] * 6 + [(32, 1)] + [(24, 1)] * 2)
    return (
        mixed_out,
        grad_text,
        grad_patches,
        grad_w_query,
        grad_w_key,
        grad_w_value,
        grad_w_out,
        vecs[16],
        vecs[17],
        vecs[13],
        vecs[11],
        vecs[12],
        grad_w_image,
        vecs[15],
        grad_c_query,
        grad_c_key,
        grad_c_value,
        grad_c_out,
        vecs[10],
        vecs[14],
        vecs[9],
        vecs[7],
        vecs[8],
        grad_w_inner,
        vecs[3:7].reshape(FF),
        grad_w_outer.astype(f32),
        vecs[2],
        vecs[0],
        vecs[1],
    )


def solution(mesh):
    items = P(AXES, None, None)
    shard, whole = P(AXES, None), P()
    in_specs = (
        (items, P(AXES), items)
        + (shard,) * 4
        + (whole,) * 5
        + (shard, whole)
        + (shard,) * 4
        + (whole,) * 5
        + (shard, whole, shard)
        + (whole,) * 3
        + (items,)
    )
    out_specs = (
        (items,) * 3
        + (shard,) * 4
        + (whole,) * 5
        + (shard, whole)
        + (shard,) * 4
        + (whole,) * 5
        + (shard, whole, shard)
        + (whole,) * 3
    )
    return jax.shard_map(local, mesh=mesh, in_specs=in_specs, out_specs=out_specs, check_vma=False)
```

```python
import jax
import jax.numpy as jnp
from jax import lax
from jax.experimental import pallas as pl
from jax.experimental.pallas import tpu as pltpu
from jax.sharding import PartitionSpec as P

D = 768
HD = 64
GROUP = 256
NGROUP = 3
PER = 4
VW = 1024
NP = 145
SEQ = 40
ITEMS = 4
TP = 48
IP = 160
TR = ITEMS * TP
IR = ITEMS * IP
FF = 3072
HALF = D // 2
CHIPS = 16
LANES = CHIPS * 2
SCALE = HD**-0.5
neg_large = -1000000000.0
ln_eps = 1e-06
bf16 = jnp.bfloat16
f32 = jnp.float32
AXES = ("mod", "dp")
MICRO = 1.1e9

Y, Z0, Z1, X = 1, 2, 4, 8
ZS = (0, Z0, Z1, Z0 | Z1)


def held_by(*masks):
    held = [0]
    for group in masks:
        held += [h ^ m for m in group for h in held]
    return held


PACKS = {
    "a": (ZS[1:], (X,), (Y,)),
    "b": (ZS[1:], (Y,), (X,)),
    "ia": ((X,), ZS[1:], (Y,)),
    "ib": ((Y,), ZS[1:], (X,)),
}


def mm(a, b):
    return jnp.dot(a, b, preferred_element_type=f32)


def mm_t(a, b):
    return lax.dot_general(a, b, (((1,), (1,)), ((), ())), preferred_element_type=f32)


def mm_w(a, b):
    return lax.dot_general(a, b, (((0,), (0,)), ((), ())), preferred_element_type=f32)


def rowsum(a):
    return jnp.sum(a.astype(f32), axis=0, keepdims=True)


def ln_parts(v):
    centered = v - jnp.mean(v, axis=-1, keepdims=True)
    spread = jnp.mean(centered * centered, axis=-1, keepdims=True)
    scale = lax.rsqrt(spread + ln_eps)
    return centered * scale, scale


def ln_back(grad, normed, scale, gain):
    a = grad * gain
    inner = a - jnp.mean(a, axis=-1, keepdims=True)
    return scale * (inner - normed * jnp.mean(a * normed, axis=-1, keepdims=True))


def head_masks():
    head = lax.broadcasted_iota(jnp.int32, (1, GROUP), 1) // HD
    return [jnp.where(head == h, 1.0, 0.0) for h in range(PER)]


def expand(rows, masks):
    return jnp.concatenate([rows * m.astype(bf16) for m in masks], axis=0)


def collapse(full, masks):
    total = full[0:TP] * masks[0]
    for h in range(1, PER):
        total = total + full[h * TP : (h + 1) * TP] * masks[h]
    return total


def softmax_rows(scores):
    e = jnp.exp(scores - jnp.max(scores, axis=-1, keepdims=True))
    return e / jnp.sum(e, axis=-1, keepdims=True)


def attend_forward(q_ref, k_ref, v_ref, o_ref, key_rows, length_of):
    masks = head_masks()
    column = lax.broadcasted_iota(jnp.int32, (1, key_rows), 1)

    def item(i, carry):
        rows = pl.ds(pl.multiple_of(i * TP, 16), TP)
        keys = pl.ds(pl.multiple_of(i * key_rows, 16), key_rows)
        bias = jnp.where(column < length_of(i), 0.0, neg_large)
        for g in range(NGROUP):
            lanes = slice(g * GROUP, (g + 1) * GROUP)
            q = expand(q_ref[rows, lanes], masks)
            probs = softmax_rows(mm_t(q, k_ref[keys, lanes]) * SCALE + bias)
            out = mm(probs.astype(bf16), v_ref[keys, lanes])
            o_ref[rows, lanes] = collapse(out, masks).astype(bf16)
        return carry

    lax.fori_loop(0, ITEMS, item, 0, unroll=True)


def attend_backward(go_ref, q_ref, k_ref, v_ref, dq_ref, dk_ref, dv_ref, key_rows, length_of):
    masks = head_masks()
    column = lax.broadcasted_iota(jnp.int32, (1, key_rows), 1)

    def item(i, carry):
        rows = pl.ds(pl.multiple_of(i * TP, 16), TP)
        keys = pl.ds(pl.multiple_of(i * key_rows, 16), key_rows)
        bias = jnp.where(column < length_of(i), 0.0, neg_large)
        for g in range(NGROUP):
            lanes = slice(g * GROUP, (g + 1) * GROUP)
            q = expand(q_ref[rows, lanes], masks)
            k = k_ref[keys, lanes]
            probs = softmax_rows(mm_t(q, k) * SCALE + bias)
            go = expand(go_ref[rows, lanes], masks)
            dp = mm_t(go, v_ref[keys, lanes])
            ds = (probs * (dp - jnp.sum(probs * dp, axis=-1, keepdims=True))).astype(bf16)
            dq_ref[rows, lanes] = (collapse(mm(ds, k), masks) * SCALE).astype(bf16)
            dk_ref[keys, lanes] = (mm_w(ds, q) * SCALE).astype(bf16)
            dv_ref[keys, lanes] = mm_w(probs.astype(bf16), go).astype(bf16)
        return carry

    lax.fori_loop(0, ITEMS, item, 0, unroll=True)


def item_bias(meta):
    column = lax.broadcasted_iota(jnp.int32, (TP, TR), 1)
    parts = []
    for i in range(ITEMS):
        inside = (column >= i * TP) & (column < i * TP + meta[2 + i])
        parts.append(jnp.where(inside, 0.0, neg_large))
    return jnp.concatenate(parts * PER, axis=0)


def gather_heads(full, masks):
    total = full[0:TR] * masks[0]
    for h in range(1, PER):
        total = total + full[h * TR : (h + 1) * TR] * masks[h]
    return total


def self_forward(q_ref, k_ref, v_ref, o_ref, meta):
    masks, bias = head_masks(), item_bias(meta)
    for g in range(NGROUP):
        lanes = slice(g * GROUP, (g + 1) * GROUP)
        q = expand(q_ref[:, lanes], masks)
        probs = softmax_rows(mm_t(q, k_ref[:, lanes]) * SCALE + bias)
        out = mm(probs.astype(bf16), v_ref[:, lanes])
        o_ref[:, lanes] = gather_heads(out, masks).astype(bf16)


def self_backward(go_ref, q_ref, k_ref, v_ref, dq_ref, dk_ref, dv_ref, meta):
    masks, bias = head_masks(), item_bias(meta)
    for g in range(NGROUP):
        lanes = slice(g * GROUP, (g + 1) * GROUP)
        q, k = expand(q_ref[:, lanes], masks), k_ref[:, lanes]
        probs = softmax_rows(mm_t(q, k) * SCALE + bias)
        go = expand(go_ref[:, lanes], masks)
        dp = mm_t(go, v_ref[:, lanes])
        ds = (probs * (dp - jnp.sum(probs * dp, axis=-1, keepdims=True))).astype(bf16)
        dq_ref[:, lanes] = (gather_heads(mm(ds, k), masks) * SCALE).astype(bf16)
        dk_ref[:, lanes] = (mm_w(ds, q) * SCALE).astype(bf16)
        dv_ref[:, lanes] = mm_w(probs.astype(bf16), go).astype(bf16)


def whole_block(x):
    zeros = (0,) * len(x.shape)
    return pl.BlockSpec(x.shape, lambda i: zeros, pipeline_mode=pl.Buffered(1))


def piece_kernel(body, name, micros, meta, weights, sizes, grads, ins, outs, far=()):
    rows = sum(sizes)
    far_in, far_out, far_scratch = far or ((), (), ())
    n_in, n_out = len(ins), len(outs)
    hbm_in = [buf for _, bufs, _, _ in weights for buf in bufs]
    n_buf = len(hbm_in)
    grad_shapes = [shape(CHIPS, rows, HALF)] * 2 if grads else []
    n_grad = len(grad_shapes)

    def kernel(*refs):
        meta_ref, refs = refs[0], refs[1:]
        in_refs, refs = refs[:n_in], refs[n_in:]
        buf_refs, refs = refs[:n_buf], refs[n_buf:]
        far_refs, refs = refs[: len(far_in)], refs[len(far_in) :]
        out_refs, refs = refs[:n_out], refs[n_out:]
        grad_refs, refs = refs[:n_grad], refs[n_grad:]
        far_refs, refs = far_refs + refs[: len(far_out)], refs[len(far_out) :]
        far_refs, refs = far_refs + refs[: len(far_scratch)], refs[len(far_scratch) :]
        if weights:
            (w_ref, load_sem), refs = refs[:2], refs[2:]
        if grads:
            g_ref, store_sem = refs
        chip, core = meta_ref[0], meta_ref[1]
        columns = [
            pl.ds(pl.multiple_of(core * HALF, 128), HALF),
            pl.ds(pl.multiple_of((1 - core) * HALF, 128), HALF),
        ]

        def load_copies():
            made, at = [], 0
            for i, (pack, _, first, count) in enumerate(weights):
                for side in range(2):
                    for j, mask in enumerate(held_by(*PACKS[pack])):
                        source = buf_refs[4 * i + side * 2 + j // 8]
                        outside = source.at[j % 8, first : first + count, :]
                        inside = w_ref.at[chip ^ mask, at : at + count, columns[side]]
                        copy = pltpu.make_async_copy(outside, inside, load_sem.at[len(made)])
                        made.append(copy)
                at += count
            return made

        def store_copies(k):
            low, pack, at = sum(sizes[:k]), None, 0
            for name_of, count in grads:
                if at <= low < at + count:
                    pack = name_of
                at += count
            rows_of, made = slice(low, low + sizes[k]), []
            for side in range(2):
                for j, mask in enumerate(held_by(*PACKS[pack])):
                    inside = g_ref.at[chip ^ mask, rows_of, columns[side]]
                    sem = store_sem.at[k * LANES + len(made)]
                    outside = grad_refs[side].at[j, rows_of, :]
                    made.append(pltpu.make_async_copy(inside, outside, sem))
            return made

        loads = load_copies() if weights else []
        stores = []
        for copy in loads:
            copy.start()

        def ready(group):
            for copy in loads[group * LANES : (group + 1) * LANES]:
                copy.wait()

        def weight(k):
            low = sum(sizes[:k])
            return w_ref[:, low : low + sizes[k], :].reshape(CHIPS * sizes[k], D)

        def put(k, value):
            low = sum(sizes[:k])
            g_ref[:, low : low + sizes[k], :] = value.astype(bf16).reshape(CHIPS, sizes[k], D)
            for copy in store_copies(k):
                copy.start()
                stores.append(copy)

        body(meta_ref, ready, weight, put, in_refs, out_refs + far_refs)
        for copy in stores:
            copy.wait()

    hbm = pl.BlockSpec(memory_space=pl.ANY)
    scratch = list(far_scratch)
    if weights:
        scratch += [
            pltpu.VMEM((CHIPS, rows, D), bf16),
            pltpu.SemaphoreType.DMA((LANES * len(weights),)),
        ]
    if grads:
        scratch += [
            pltpu.VMEM((CHIPS, rows, D), bf16),
            pltpu.SemaphoreType.DMA((LANES * len(sizes),)),
        ]
    made = pl.pallas_call(
        kernel,
        out_shape=list(outs) + grad_shapes + list(far_out),
        grid=(1,),
        in_specs=[pl.BlockSpec(memory_space=pltpu.SMEM)]
        + [whole_block(x) for x in ins]
        + [hbm] * (n_buf + len(far_in)),
        out_specs=[whole_block(x) for x in outs] + [hbm] * (n_grad + len(far_out)),
        scratch_shapes=scratch,
        compiler_params=pltpu.CompilerParams(vmem_limit_bytes=(60 if far_in else 50) * 1024 * 1024),
        cost_estimate=pl.CostEstimate(
            flops=int(micros * MICRO), bytes_accessed=0, transcendentals=0
        ),
        name=name,
    )(meta, *ins, *hbm_in, *far_in)
    return made[:n_out], made[n_out:]


PARAMS = (
    "b_query",
    "b_value",
    "b_out",
    "gain_one",
    "bias_one",
    "b_image",
    "cb_query",
    "cb_value",
    "cb_out",
    "gain_two",
    "bias_two",
    "b_outer",
    "gain_three",
    "bias_three",
)
B_INNER = 16


def param(ref, name):
    at = PARAMS.index(name)
    return ref[at : at + 1]


def join_params(*vectors):
    def kernel(*refs):
        out = refs[-1]
        for i, ref in enumerate(refs[:-2]):
            out[i : i + 1] = ref[...].reshape(1, D)
        out[len(PARAMS) : B_INNER] = jnp.zeros((B_INNER - len(PARAMS), D), f32)
        inner = refs[-2][...].reshape(1, FF)
        for k in range(4):
            out[B_INNER + k : B_INNER + k + 1] = inner[:, k * D : (k + 1) * D]
        out[B_INNER + 4 :] = jnp.zeros((4, D), f32)

    vmem = pl.BlockSpec(memory_space=pltpu.VMEM)
    return pl.pallas_call(
        kernel,
        out_shape=shape(24, D, dtype=f32),
        in_specs=[vmem] * len(vectors),
        out_specs=vmem,
        name="join_params",
    )(*vectors)


def pack_shards(core, shards):
    rows = sum(s.shape[0] * (s.shape[1] // D) for s in shards)

    def kernel(core_ref, *refs):
        parts = []
        for ref in refs[:-2]:
            full = ref[...].astype(f32)
            parts += [full[:, k * D : (k + 1) * D] for k in range(full.shape[1] // D)]
        full = jnp.concatenate(parts, axis=0)
        second = core_ref[0] > 0
        low, high = full[:, :HALF], full[:, HALF:]
        refs[-2][...] = jnp.where(second, high, low).astype(bf16)
        refs[-1][...] = jnp.where(second, low, high).astype(bf16)

    vmem = pl.BlockSpec(memory_space=pltpu.VMEM)
    return pl.pallas_call(
        kernel,
        out_shape=[shape(rows, HALF)] * 2,
        in_specs=[pl.BlockSpec(memory_space=pltpu.SMEM)] + [vmem] * len(shards),
        out_specs=[vmem] * 2,
        name="pack_shards",
    )(core[None].astype(jnp.int32), *shards)


def small_call(kernel, name, core, ins, outs):
    vmem = pl.BlockSpec(memory_space=pltpu.VMEM)
    return pl.pallas_call(
        kernel,
        out_shape=outs,
        in_specs=[pl.BlockSpec(memory_space=pltpu.SMEM)] + [vmem] * len(ins),
        out_specs=[vmem] * len(outs),
        name=name,
    )(core[None].astype(jnp.int32), *ins)


def split_cores(core, pieces):
    rows = sum(sum(sizes) for _, sizes in pieces) // 2

    def kernel(core_ref, *refs):
        second = core_ref[0] > 0
        out = 0
        for i, (_, sizes) in enumerate(pieces):
            total = refs[4 * i][...].astype(f32)
            for ref in refs[4 * i + 1 : 4 * i + 4]:
                total = total + ref[...].astype(f32)
            at = 0
            for size in sizes:
                half = size // 2
                low, high = total[at : at + half], total[at + half : at + size]
                refs[-2][out : out + half] = jnp.where(second, high, low)
                refs[-1][out : out + half] = jnp.where(second, low, high)
                at, out = at + size, out + half

    ins = [term for terms, _ in pieces for term in terms]
    return small_call(kernel, "split_cores", core, ins, [shape(rows, HALF, dtype=f32)] * 2)


def join_halves(core, mine, came, counts):
    def kernel(core_ref, mine_ref, came_ref, *outs):
        second, at = core_ref[0] > 0, 0
        for out, (rows, wide) in zip(outs, counts):
            for k in range(wide):
                a, b = mine_ref[at : at + rows], came_ref[at : at + rows]
                out[:, k * D : k * D + HALF] = jnp.where(second, b, a)
                out[:, k * D + HALF : (k + 1) * D] = jnp.where(second, a, b)
                at += rows

    outs = [shape(rows, wide * D, dtype=f32) for rows, wide in counts]
    return small_call(kernel, "join_halves", core, [mine, came], outs)


def shape(*dims, dtype=bf16):
    return jax.ShapeDtypeStruct(dims, dtype)


def first_front(meta, ready, weight, put, ins, outs):
    text, images, params = ins
    q, k, v, attn, image_rows, ck, cv = outs
    ready(0)
    rows = text[:TR]
    q[...] = (mm(rows, weight(0)) + param(params, "b_query")).astype(bf16)
    k[...] = mm(rows, weight(1)).astype(bf16)
    v[...] = (mm(rows, weight(2)) + param(params, "b_value")).astype(bf16)
    self_forward(q, k, v, attn, meta)
    ready(1)
    image_rows[...] = (mm(images[...], weight(3)) + param(params, "b_image")).astype(bf16)
    ck[...] = mm(image_rows[...], weight(4)).astype(bf16)
    cv[...] = (mm(image_rows[...], weight(5)) + param(params, "cb_value")).astype(bf16)


def mid_front(meta, ready, weight, put, ins, outs):
    text, attn, ck, cv, params = ins
    hidden, cq, cross, joint, sum_one, sum_two = outs
    ready(0)
    ready(1)
    sum_one[...] = text[:TR].astype(f32) + (mm(attn[...], weight(0)) + param(params, "b_out"))
    normed, _ = ln_parts(sum_one[...])
    hidden[...] = (normed * param(params, "gain_one") + param(params, "bias_one")).astype(bf16)
    cq[...] = (mm(hidden[...], weight(1)) + param(params, "cb_query")).astype(bf16)
    attend_forward(cq, ck, cv, cross, IP, lambda i: NP)
    sum_two[...] = hidden[...].astype(f32) + (mm(cross[...], weight(2)) + param(params, "cb_out"))
    normed, _ = ln_parts(sum_two[...])
    joint[...] = (normed * param(params, "gain_two") + param(params, "bias_two")).astype(bf16)


def feed_forward(meta, ready, weight, put, ins, outs):
    joint, cot, sum_two, params = ins
    mixed, grad_sum_two, vec_three, vec_two = outs[:4]
    outer_hbm, grad_outer_hbm, outer_w, grad_outer_w, active, slope, grad_inner, sem = outs[4:]
    load = pltpu.make_async_copy(outer_hbm, outer_w, sem.at[0])
    load.start()
    ready(0)
    ready(1)
    for k in range(4):
        lanes = slice(k * D, (k + 1) * D)
        pre = mm(joint[...], weight(k)) + params[B_INNER + k : B_INNER + k + 1]
        cdf = 0.5 * (1.0 + lax.erf(pre * 0.5**0.5))
        active[:, lanes] = (pre * cdf).astype(bf16)
        slope[:, lanes] = cdf + pre * (jnp.exp(-0.5 * pre * pre) * 0.3989422804014327)
    load.wait()
    outer = mm(active[...], outer_w[...]) + param(params, "b_outer")
    normed, scale = ln_parts(joint[...].astype(f32) + outer)
    gain = param(params, "gain_three")
    result = normed * gain + param(params, "bias_three")
    row = lax.broadcasted_iota(jnp.int32, (TP, 1), 0)
    keep = [jnp.where(row < meta[2 + i], 1.0, 0.0) for i in range(ITEMS)]
    for i in range(ITEMS):
        mixed[i] = (result[i * TP : (i + 1) * TP] * keep[i])[:SEQ]
    grad = cot[...].astype(f32) * jnp.concatenate(keep, axis=0)
    grad_sum = ln_back(grad, normed, scale, gain)
    grad_outer = grad_sum.astype(bf16)
    vec_three[0:1] = rowsum(grad * normed)
    vec_three[1:2] = rowsum(grad)
    vec_three[2:3] = rowsum(grad_outer)
    vec_three[3:4] = jnp.zeros((1, D), f32)
    grad_outer_w[...] = mm_w(active[...], grad_outer).astype(bf16)
    store = pltpu.make_async_copy(grad_outer_w, grad_outer_hbm, sem.at[1])
    store.start()
    for k in range(4):
        lanes = slice(k * D, (k + 1) * D)
        part = (slope[:, lanes] * mm_t(grad_outer, outer_w[lanes, :])).astype(bf16)
        grad_inner[:, lanes] = part
        vec_three[4 + k : 5 + k] = rowsum(part)
        put(k, mm_w(joint[...], part))
    grad = grad_sum
    for k in range(4):
        grad = grad + mm_t(grad_inner[:, k * D : (k + 1) * D], weight(k))
    normed, scale = ln_parts(sum_two[...])
    grad_sum_two[...] = ln_back(grad, normed, scale, param(params, "gain_two"))
    vec_two[...] = jnp.concatenate(
        [rowsum(grad * normed), rowsum(grad), jnp.zeros((6, D), f32)], axis=0
    )
    store.wait()


def mid_back(meta, ready, weight, put, ins, outs):
    grad_sum_two, cross, hidden, attn, cq, ck, cv, sum_one, params = ins
    grad_sum_one, grad_attn, dk, dv, vec, dq, grad_cross = outs
    gain = param(params, "gain_one")
    grad_cross_branch = grad_sum_two[...].astype(bf16)
    ready(0)
    ready(1)
    grad_cross[...] = mm_t(grad_cross_branch, weight(2)).astype(bf16)
    attend_backward(grad_cross, cq, ck, cv, dq, dk, dv, IP, lambda i: NP)
    put(2, mm_w(cross[...], grad_cross_branch))
    put(1, mm_w(hidden[...], dq[...]))
    grad = grad_sum_two[...] + mm_t(dq[...], weight(1))
    normed, scale = ln_parts(sum_one[...])
    grad_sum_one[...] = ln_back(grad, normed, scale, gain)
    grad_branch = grad_sum_one[...].astype(bf16)
    put(0, mm_w(attn[...], grad_branch))
    grad_attn[...] = mm_t(grad_branch, weight(0)).astype(bf16)
    vec[...] = jnp.concatenate(
        [
            rowsum(grad_cross_branch),
            rowsum(dq[...]),
            rowsum(grad * normed),
            rowsum(grad),
            rowsum(grad_branch),
            jnp.zeros((3, D), f32),
        ],
        axis=0,
    )


def image_back(meta, ready, weight, put, ins, outs):
    images, image_rows, dk, dv = ins
    grad_patches, vec = outs
    put(1, mm_w(image_rows[...], dk[...]))
    put(2, mm_w(image_rows[...], dv[...]))
    ready(0)
    grad_image = (mm_t(dk[...], weight(1)) + mm_t(dv[...], weight(2))).astype(bf16)
    put(0, mm_w(images[...], grad_image))
    for i in range(ITEMS):
        grad_patches[i] = mm_t(grad_image[i * IP : (i + 1) * IP], weight(0))[:NP]
    vec[...] = jnp.concatenate([rowsum(dv[...]), rowsum(grad_image), jnp.zeros((6, D), f32)], axis=0)


def self_back(meta, ready, weight, put, ins, outs):
    grad_attn, q, k, v, text, grad_sum_one = ins
    grad_text, vec, dq, dk, dv = outs
    self_backward(grad_attn, q, k, v, dq, dk, dv, meta)
    put(0, mm_w(text[:TR], dq[...]))
    put(1, mm_w(text[:TR], dk[...]))
    put(2, mm_w(text[:TR], dv[...]))
    ready(0)
    total = grad_sum_one[...] + mm_t(dq[...], weight(0))
    total = total + mm_t(dk[...], weight(1))
    grad_text[...] = (total + mm_t(dv[...], weight(2))).astype(bf16)
    vec[...] = jnp.concatenate([rowsum(dq[...]), rowsum(dv[...]), jnp.zeros((6, D), f32)], axis=0)


def local(
    text,
    lengths,
    patches,
    w_query,
    w_key,
    w_value,
    w_out,
    b_query,
    b_value,
    b_out,
    gain_one,
    bias_one,
    w_image,
    b_image,
    c_query,
    c_key,
    c_value,
    c_out,
    cb_query,
    cb_value,
    cb_out,
    gain_two,
    bias_two,
    w_inner,
    b_inner,
    w_outer,
    b_outer,
    gain_three,
    bias_three,
    cotangent,
):
    count = lax.axis_size("mod") * lax.axis_size("dp")
    fold = count // LANES
    device = lax.axis_index("mod") * lax.axis_size("dp") + lax.axis_index("dp")
    place = device // fold
    core, chip = place % 2, place // 2
    first_core = core == 0

    def flip_device(block, mask):
        return lax.ppermute(block, AXES, [(i, i ^ mask) for i in range(count)])

    def flip_chip(block, mask):
        return flip_device(block, mask * 2 * fold)

    def flip_core(block):
        return flip_device(block, fold)

    def swap(block):
        return lax.ppermute(block, "mod", [(0, 1), (1, 0)])

    def gather_fold(shard):
        step = 1
        while step < fold:
            other = flip_device(shard, step)
            low = (device // step) % 2 == 0
            shard = jnp.concatenate(
                [jnp.where(low, shard, other), jnp.where(low, other, shard)], axis=0
            )
            step *= 2
        return shard

    def scatter_fold(total):
        step = fold // 2
        while step >= 1:
            low = (device // step) % 2 == 0
            half = total.shape[0] // 2
            kept = jnp.where(low, total[:half], total[half:])
            total = kept + flip_device(jnp.where(low, total[half:], total[:half]), step)
            step //= 2
        return total

    def split_rows(blocks, sizes):
        at, parts = 0, []
        for size in sizes:
            parts.append(blocks[..., at : at + size, :])
            at += size
        return parts

    def own_blocks(groups):
        kept, sent = pack_shards(core, [gather_fold(s) for g in groups for s in g])
        came = flip_core(sent)
        lows, highs = jnp.where(first_core, kept, came), jnp.where(first_core, came, kept)
        blocks, at = [], 0
        for g in groups:
            parts = []
            for shard in g:
                for _ in range(shard.shape[1] // D):
                    count = shard.shape[0] * fold
                    parts += [lows[at : at + count], highs[at : at + count]]
                    at += count
            blocks.append(jnp.concatenate(parts, axis=0))
        return blocks

    def spread(blocks, masks):
        return [flip_chip(blocks, m) for m in masks]

    def reduce_core(bufs):
        return [bufs[0], flip_core(bufs[1])]

    def add(*terms):
        return sum(t.astype(f32) for t in terms)

    def reduce_last(groups, terms):
        at, far = 0, []
        for pack, count in groups:
            out = add(*[t[8:, at : at + count] for t in terms]).astype(bf16)
            far.append(flip_chip(out, PACKS[pack][2][0]))
            at += count
        return far

    def parts_of(groups, terms, far):
        at, parts = 0, []
        for (pack, count), came in zip(groups, far):

            def total(low, high, at=at, count=count, came=came):
                return add(*[t[low:high, at : at + count] for t in terms], came[low:high])

            parts.append((pack, total))
            at += count
        return parts

    def reduce_across(parts):
        blocks = []
        for pack in ("a", "b"):
            totals = [total for name, total in parts if name == pack]
            sent = jnp.concatenate([t(4, 8).astype(bf16) for t in totals], axis=1)
            blocks.append(flip_chip(sent, PACKS[pack][1][0]))
        return blocks

    def four_blocks(parts, across):
        blocks = []
        for pack, came in zip(("a", "b"), across):
            kept = jnp.concatenate([total(0, 4) for name, total in parts if name == pack], axis=1)
            blocks.append(add(kept, came).astype(bf16))
        return jnp.concatenate(blocks, axis=1)

    def reduce_z(blocks):
        return [blocks[0]] + [flip_chip(blocks[j], ZS[j]) for j in range(1, 4)]

    def finish(pieces, counts):
        mine, theirs = split_cores(core, pieces)
        return [scatter_fold(w) for w in join_halves(core, mine, flip_core(theirs), counts)]

    def sum_near(total):
        step = 1
        while step <= fold:
            total = total + flip_device(total, step)
            step *= 2
        return total

    def hold(values, *after):
        count = len(values)
        return list(lax.optimization_barrier(tuple(values) + after)[:count])

    text_rows = jnp.pad(text, ((0, 0), (0, TP - SEQ), (0, 0))).reshape(TR, D)
    lengths_row = jnp.pad(lengths.astype(bf16)[None], ((0, 15), (0, D - ITEMS)))
    text_rows = swap(jnp.concatenate([text_rows, lengths_row], axis=0))
    item_lengths = text_rows[TR, :ITEMS]
    cot_rows = jnp.pad(cotangent, ((0, 0), (0, TP - SEQ), (0, 0))).reshape(TR, D)
    meta = jnp.concatenate([chip[None], core[None], item_lengths.astype(jnp.int32)]).astype(jnp.int32)
    images = jnp.pad(patches, ((0, 0), (0, IP - NP), (0, 0))).reshape(IR, VW)
    params = join_params(
        *(b_query, b_value, b_out, gain_one, bias_one, b_image, cb_query),
        *(cb_value, cb_out, gain_two, bias_two, b_outer, gain_three, bias_three, b_inner),
    )
    w_outer = lax.all_gather(w_outer, AXES, axis=0, tiled=True)
    first, middle = own_blocks(
        [[w_query, w_key, w_value, c_query, c_out, w_image, c_key, c_value, w_out], [w_inner]]
    )
    first = jnp.stack([first] + spread(first, ZS[1:]))
    ma = jnp.stack([middle[:96], flip_chip(middle[:96], X)])
    mb = jnp.stack([middle[96:], flip_chip(middle[96:], Y)])
    middle = jnp.concatenate([ma, mb], axis=1)
    middle = jnp.concatenate([middle, flip_chip(middle, Z0)])
    a_4, b_4, ma, mb = hold(
        [first[:, :240], first[:, 240:], middle[:, :96], middle[:, 96:]], text_rows
    )
    a_8 = jnp.concatenate([a_4, flip_chip(a_4, X)])
    b_8 = jnp.concatenate([b_4, flip_chip(b_4, Y)])
    ma = jnp.concatenate([ma, flip_chip(ma, Z1)])
    a_8, b_8, ma, mb = hold([a_8, b_8, ma, mb])
    mb = jnp.concatenate([mb, flip_chip(mb, Z1)])
    a_far, b_far = flip_chip(a_8, Y), flip_chip(b_8, X)
    a_side, b_side = flip_core(a_8), flip_core(b_8)
    ma, mb, a_far, b_far, cot_rows = hold([ma, mb, a_far, b_far, cot_rows], a_side, b_side)
    cot_rows = swap(cot_rows)
    pack_a = [a_8, a_far, a_side, flip_core(a_far)]
    pack_b = [b_8, b_far, b_side, flip_core(b_far)]
    ma_far, mb_far = flip_chip(ma, Y), flip_chip(mb, X)
    qkv, img = ("a", pack_a, 0, 144), ("b", pack_b, 0, 160)
    mid = [("b", pack_b, 160, 48), ("a", pack_a, 144, 96)]
    qkv_sizes, img_sizes, mid_sizes = (48,) * 3, (64, 48, 48), (48,) * 3
    inner_sizes = (48,) * 4

    text_shape, image_shape = shape(TR, D), shape(IR, D)
    wide = shape(TR, D, dtype=f32)
    vec_shape = shape(8, D, dtype=f32)
    (q, k, v, attn, image_rows, ck, cv), _ = piece_kernel(
        first_front,
        "first_front",
        10,
        meta,
        [qkv, img],
        qkv_sizes + img_sizes,
        [],
        [text_rows, images, params],
        [text_shape] * 4 + [image_shape] * 3,
    )
    ma, mb, ma_far, mb_far, image_rows = hold([ma, mb, ma_far, mb_far, image_rows])
    inner = [
        ("ia", [ma, ma_far, flip_core(ma), flip_core(ma_far)], 0, 96),
        ("ib", [mb, mb_far, flip_core(mb), flip_core(mb_far)], 0, 96),
    ]
    (hidden, cq, cross, joint, sum_one, sum_two), _ = piece_kernel(
        mid_front,
        "mid_front",
        6,
        meta,
        mid,
        mid_sizes,
        [],
        [text_rows, attn, ck, cv, params],
        [text_shape] * 4 + [wide] * 2,
    )
    inner_groups, mid_groups = [("a", 96), ("b", 96)], [("b", 96), ("a", 48)]
    img_groups, qkv_groups = [("b", 160)], [("a", 144)]
    (mixed, grad_sum_two, vec_outer, vec_inner), (*inner_bufs, grad_w_outer) = piece_kernel(
        feed_forward,
        "feed_forward",
        17,
        meta,
        inner,
        inner_sizes,
        inner_groups,
        [joint, cot_rows, sum_two, params],
        [shape(ITEMS, SEQ, D, dtype=f32), wide, vec_shape, vec_shape],
        (
            [w_outer],
            [shape(FF, D)],
            [pltpu.VMEM((FF, D), bf16)] * 2
            + [pltpu.VMEM((TR, FF), bf16), pltpu.VMEM((TR, FF), f32), pltpu.VMEM((TR, FF), bf16)]
            + [pltpu.SemaphoreType.DMA((2,))],
        ),
    )
    grad_w_outer = lax.psum_scatter(grad_w_outer, AXES, scatter_dimension=0, tiled=True)
    inner_terms = reduce_core(inner_bufs)
    (grad_sum_one, grad_attn, dk, dv, vec_mid), mid_bufs = piece_kernel(
        mid_back,
        "mid_back",
        14,
        meta,
        mid,
        mid_sizes,
        mid_groups,
        [grad_sum_two, cross, hidden, attn, cq, ck, cv, sum_one, params],
        [wide, text_shape, image_shape, image_shape, vec_shape],
        ((), (), [pltpu.VMEM((TR, D), bf16)] * 2),
    )
    dk, mixed_out, *inner_terms = hold([dk, swap(mixed), *inner_terms])
    inner_far = reduce_last(inner_groups, inner_terms)
    mid_terms = reduce_core(mid_bufs)
    (grad_patches, vec_image), img_bufs = piece_kernel(
        image_back,
        "image_back",
        12,
        meta,
        [img],
        img_sizes,
        img_groups,
        [images, image_rows, dk, dv],
        [shape(ITEMS, NP, VW, dtype=f32), vec_shape],
    )
    img_terms = reduce_core(img_bufs)
    grad_attn, *held = hold([grad_attn, vec_image, *mid_terms, *inner_far])
    vec_image, mid_terms, inner_far = held[0], held[1:3], held[3:]
    mid_far = reduce_last(mid_groups, mid_terms)
    inner_parts = parts_of(inner_groups, inner_terms, inner_far)
    inner_across = reduce_across(inner_parts)
    (grad_text, vec_self), qkv_bufs = piece_kernel(
        self_back,
        "self_back",
        13,
        meta,
        [qkv],
        qkv_sizes,
        qkv_groups,
        [grad_attn, q, k, v, text_rows, grad_sum_one],
        [text_shape, vec_shape],
        ((), (), [pltpu.VMEM((TR, D), bf16)] * 3),
    )
    grad_patches, *held = hold(
        [grad_patches, vec_self, *qkv_bufs, *img_terms, *mid_far, *inner_across]
    )
    vec_self, qkv_bufs, img_terms = held[0], held[1:3], held[3:5]
    mid_far, inner_across = held[5:7], held[7:]
    qkv_terms = reduce_core(qkv_bufs)
    both_far = reduce_last(img_groups, img_terms) + reduce_last(qkv_groups, qkv_terms)
    rows = [vec_outer[:3], vec_outer[4:8], vec_inner[:2], vec_mid[:5], vec_image[:2], vec_self[:2]]
    vecs = sum_near(jnp.concatenate(rows + [jnp.zeros((6, D), f32)], axis=0))
    vecs = sum([flip_chip(vecs, z) for z in ZS[1:]], vecs)
    inner_blocks = four_blocks(inner_parts, inner_across)
    inner_blocks, vecs, *both_far = hold([inner_blocks, vecs, *both_far])
    parts = (
        parts_of(mid_groups, mid_terms, mid_far)
        + parts_of(img_groups, img_terms, both_far[:1])
        + parts_of(qkv_groups, qkv_terms, both_far[1:])
    )
    across = reduce_across(parts)
    inner_terms = reduce_z(inner_blocks)
    vecs, grad_text, *held = hold([vecs, grad_text, *across, *inner_terms])
    across, inner_terms = held[:2], held[2:]
    terms = reduce_z(four_blocks(parts, across))
    vecs = sum([flip_chip(vecs, m) for m in (X, Y, X | Y)], vecs)
    grad_text = swap(grad_text).reshape(ITEMS, TP, D)[:, :SEQ].astype(f32)
    vecs, *inner_terms = hold([vecs, *inner_terms])
    (grad_w_inner,) = finish([(inner_terms, inner_sizes)], [(24, 4)])
    (
        grad_c_out,
        grad_w_query,
        grad_w_key,
        grad_w_value,
        grad_w_out,
        grad_c_query,
        grad_w_image,
        grad_c_key,
        grad_c_value,
    ) = finish([(terms, (48,) * 6 + img_sizes)], [(24, 1)] * 6 + [(32, 1)] + [(24, 1)] * 2)
    return (
        mixed_out,
        grad_text,
        grad_patches,
        grad_w_query,
        grad_w_key,
        grad_w_value,
        grad_w_out,
        vecs[16],
        vecs[17],
        vecs[13],
        vecs[11],
        vecs[12],
        grad_w_image,
        vecs[15],
        grad_c_query,
        grad_c_key,
        grad_c_value,
        grad_c_out,
        vecs[10],
        vecs[14],
        vecs[9],
        vecs[7],
        vecs[8],
        grad_w_inner,
        vecs[3:7].reshape(FF),
        grad_w_outer.astype(f32),
        vecs[2],
        vecs[0],
        vecs[1],
    )


def solution(mesh):
    items = P(AXES, None, None)
    shard, whole = P(AXES, None), P()
    in_specs = (
        (items, P(AXES), items)
        + (shard,) * 4
        + (whole,) * 5
        + (shard, whole)
        + (shard,) * 4
        + (whole,) * 5
        + (shard, whole, shard)
        + (whole,) * 3
        + (items,)
    )
    out_specs = (
        (items,) * 3
        + (shard,) * 4
        + (whole,) * 5
        + (shard, whole)
        + (shard,) * 4
        + (whole,) * 5
        + (shard, whole, shard)
        + (whole,) * 3
    )
    return jax.shard_map(local, mesh=mesh, in_specs=in_specs, out_specs=out_specs, check_vma=False)
```

```python
import jax
import jax.numpy as jnp
from jax import lax
from jax.experimental import pallas as pl
from jax.experimental.pallas import tpu as pltpu
from jax.sharding import PartitionSpec as P

D = 768
HD = 64
GROUP = 256
NGROUP = 3
PER = 4
VW = 1024
NP = 145
SEQ = 40
ITEMS = 4
TP = 48
IP = 160
TR = ITEMS * TP
IR = ITEMS * IP
FF = 3072
HALF = D // 2
CHIPS = 16
LANES = CHIPS * 2
SCALE = HD**-0.5
neg_large = -1000000000.0
ln_eps = 1e-06
bf16 = jnp.bfloat16
f32 = jnp.float32
AXES = ("mod", "dp")
MICRO = 1.1e9

Y, Z0, Z1, X = 1, 2, 4, 8
ZS = (0, Z0, Z1, Z0 | Z1)


def held_by(*masks):
    held = [0]
    for group in masks:
        held += [h ^ m for m in group for h in held]
    return held


PACKS = {
    "a": (ZS[1:], (X,), (Y,)),
    "b": (ZS[1:], (Y,), (X,)),
    "ia": ((X,), ZS[1:], (Y,)),
    "ib": ((Y,), ZS[1:], (X,)),
}


def mm(a, b):
    return jnp.dot(a, b, preferred_element_type=f32)


def mm_t(a, b):
    return lax.dot_general(a, b, (((1,), (1,)), ((), ())), preferred_element_type=f32)


def mm_w(a, b):
    return lax.dot_general(a, b, (((0,), (0,)), ((), ())), preferred_element_type=f32)


def rowsum(a):
    return jnp.sum(a.astype(f32), axis=0, keepdims=True)


def ln_parts(v):
    centered = v - jnp.mean(v, axis=-1, keepdims=True)
    spread = jnp.mean(centered * centered, axis=-1, keepdims=True)
    scale = lax.rsqrt(spread + ln_eps)
    return centered * scale, scale


def ln_back(grad, normed, scale, gain):
    a = grad * gain
    inner = a - jnp.mean(a, axis=-1, keepdims=True)
    return scale * (inner - normed * jnp.mean(a * normed, axis=-1, keepdims=True))


def head_masks():
    head = lax.broadcasted_iota(jnp.int32, (1, GROUP), 1) // HD
    return [jnp.where(head == h, 1.0, 0.0) for h in range(PER)]


def expand(rows, masks):
    return jnp.concatenate([rows * m.astype(bf16) for m in masks], axis=0)


def collapse(full, masks):
    total = full[0:TP] * masks[0]
    for h in range(1, PER):
        total = total + full[h * TP : (h + 1) * TP] * masks[h]
    return total


def softmax_rows(scores):
    e = jnp.exp(scores - jnp.max(scores, axis=-1, keepdims=True))
    return e / jnp.sum(e, axis=-1, keepdims=True)


def attend_forward(q_ref, k_ref, v_ref, o_ref, key_rows, length_of):
    masks = head_masks()
    column = lax.broadcasted_iota(jnp.int32, (1, key_rows), 1)

    def item(i, carry):
        rows = pl.ds(pl.multiple_of(i * TP, 16), TP)
        keys = pl.ds(pl.multiple_of(i * key_rows, 16), key_rows)
        bias = jnp.where(column < length_of(i), 0.0, neg_large)
        for g in range(NGROUP):
            lanes = slice(g * GROUP, (g + 1) * GROUP)
            q = expand(q_ref[rows, lanes], masks)
            probs = softmax_rows(mm_t(q, k_ref[keys, lanes]) * SCALE + bias)
            out = mm(probs.astype(bf16), v_ref[keys, lanes])
            o_ref[rows, lanes] = collapse(out, masks).astype(bf16)
        return carry

    lax.fori_loop(0, ITEMS, item, 0, unroll=True)


def attend_backward(go_ref, q_ref, k_ref, v_ref, dq_ref, dk_ref, dv_ref, key_rows, length_of):
    masks = head_masks()
    column = lax.broadcasted_iota(jnp.int32, (1, key_rows), 1)

    def item(i, carry):
        rows = pl.ds(pl.multiple_of(i * TP, 16), TP)
        keys = pl.ds(pl.multiple_of(i * key_rows, 16), key_rows)
        bias = jnp.where(column < length_of(i), 0.0, neg_large)
        for g in range(NGROUP):
            lanes = slice(g * GROUP, (g + 1) * GROUP)
            q = expand(q_ref[rows, lanes], masks)
            k = k_ref[keys, lanes]
            probs = softmax_rows(mm_t(q, k) * SCALE + bias)
            go = expand(go_ref[rows, lanes], masks)
            dp = mm_t(go, v_ref[keys, lanes])
            ds = (probs * (dp - jnp.sum(probs * dp, axis=-1, keepdims=True))).astype(bf16)
            dq_ref[rows, lanes] = (collapse(mm(ds, k), masks) * SCALE).astype(bf16)
            dk_ref[keys, lanes] = (mm_w(ds, q) * SCALE).astype(bf16)
            dv_ref[keys, lanes] = mm_w(probs.astype(bf16), go).astype(bf16)
        return carry

    lax.fori_loop(0, ITEMS, item, 0, unroll=True)


def item_bias(meta):
    column = lax.broadcasted_iota(jnp.int32, (TP, TR), 1)
    parts = []
    for i in range(ITEMS):
        inside = (column >= i * TP) & (column < i * TP + meta[2 + i])
        parts.append(jnp.where(inside, 0.0, neg_large))
    return jnp.concatenate(parts * PER, axis=0)


def gather_heads(full, masks):
    total = full[0:TR] * masks[0]
    for h in range(1, PER):
        total = total + full[h * TR : (h + 1) * TR] * masks[h]
    return total


def self_forward(q_ref, k_ref, v_ref, o_ref, meta):
    masks, bias = head_masks(), item_bias(meta)
    for g in range(NGROUP):
        lanes = slice(g * GROUP, (g + 1) * GROUP)
        q = expand(q_ref[:, lanes], masks)
        probs = softmax_rows(mm_t(q, k_ref[:, lanes]) * SCALE + bias)
        out = mm(probs.astype(bf16), v_ref[:, lanes])
        o_ref[:, lanes] = gather_heads(out, masks).astype(bf16)


def self_backward(go_ref, q_ref, k_ref, v_ref, dq_ref, dk_ref, dv_ref, meta):
    masks, bias = head_masks(), item_bias(meta)
    for g in range(NGROUP):
        lanes = slice(g * GROUP, (g + 1) * GROUP)
        q, k = expand(q_ref[:, lanes], masks), k_ref[:, lanes]
        probs = softmax_rows(mm_t(q, k) * SCALE + bias)
        go = expand(go_ref[:, lanes], masks)
        dp = mm_t(go, v_ref[:, lanes])
        ds = (probs * (dp - jnp.sum(probs * dp, axis=-1, keepdims=True))).astype(bf16)
        dq_ref[:, lanes] = (gather_heads(mm(ds, k), masks) * SCALE).astype(bf16)
        dk_ref[:, lanes] = (mm_w(ds, q) * SCALE).astype(bf16)
        dv_ref[:, lanes] = mm_w(probs.astype(bf16), go).astype(bf16)


def whole_block(x):
    zeros = (0,) * len(x.shape)
    return pl.BlockSpec(x.shape, lambda i: zeros, pipeline_mode=pl.Buffered(1))


def piece_kernel(body, name, micros, meta, weights, sizes, grads, ins, outs, far=()):
    rows = sum(sizes)
    far_in, far_out, far_scratch = far or ((), (), ())
    n_in, n_out = len(ins), len(outs)
    hbm_in = [buf for _, bufs, _, _ in weights for buf in bufs]
    n_buf = len(hbm_in)
    grad_shapes = [shape(CHIPS, rows, HALF)] * 2 if grads else []
    n_grad = len(grad_shapes)

    def kernel(*refs):
        meta_ref, refs = refs[0], refs[1:]
        in_refs, refs = refs[:n_in], refs[n_in:]
        buf_refs, refs = refs[:n_buf], refs[n_buf:]
        far_refs, refs = refs[: len(far_in)], refs[len(far_in) :]
        out_refs, refs = refs[:n_out], refs[n_out:]
        grad_refs, refs = refs[:n_grad], refs[n_grad:]
        far_refs, refs = far_refs + refs[: len(far_out)], refs[len(far_out) :]
        far_refs, refs = far_refs + refs[: len(far_scratch)], refs[len(far_scratch) :]
        if weights:
            (w_ref, load_sem), refs = refs[:2], refs[2:]
        if grads:
            g_ref, store_sem = refs
        chip, core = meta_ref[0], meta_ref[1]
        columns = [
            pl.ds(pl.multiple_of(core * HALF, 128), HALF),
            pl.ds(pl.multiple_of((1 - core) * HALF, 128), HALF),
        ]

        def load_copies():
            made, at = [], 0
            for i, (pack, _, first, count) in enumerate(weights):
                for side in range(2):
                    for j, mask in enumerate(held_by(*PACKS[pack])):
                        source = buf_refs[4 * i + side * 2 + j // 8]
                        outside = source.at[j % 8, first : first + count, :]
                        inside = w_ref.at[chip ^ mask, at : at + count, columns[side]]
                        copy = pltpu.make_async_copy(outside, inside, load_sem.at[len(made)])
                        made.append(copy)
                at += count
            return made

        def store_copies(k):
            low, pack, at = sum(sizes[:k]), None, 0
            for name_of, count in grads:
                if at <= low < at + count:
                    pack = name_of
                at += count
            rows_of, made = slice(low, low + sizes[k]), []
            for side in range(2):
                for j, mask in enumerate(held_by(*PACKS[pack])):
                    inside = g_ref.at[chip ^ mask, rows_of, columns[side]]
                    sem = store_sem.at[k * LANES + len(made)]
                    outside = grad_refs[side].at[j, rows_of, :]
                    made.append(pltpu.make_async_copy(inside, outside, sem))
            return made

        loads = load_copies() if weights else []
        stores = []
        for copy in loads:
            copy.start()

        def ready(group):
            for copy in loads[group * LANES : (group + 1) * LANES]:
                copy.wait()

        def weight(k):
            low = sum(sizes[:k])
            return w_ref[:, low : low + sizes[k], :].reshape(CHIPS * sizes[k], D)

        def put(k, value):
            low = sum(sizes[:k])
            g_ref[:, low : low + sizes[k], :] = value.astype(bf16).reshape(CHIPS, sizes[k], D)
            for copy in store_copies(k):
                copy.start()
                stores.append(copy)

        body(meta_ref, ready, weight, put, in_refs, out_refs + far_refs)
        for copy in stores:
            copy.wait()

    hbm = pl.BlockSpec(memory_space=pl.ANY)
    scratch = list(far_scratch)
    if weights:
        scratch += [
            pltpu.VMEM((CHIPS, rows, D), bf16),
            pltpu.SemaphoreType.DMA((LANES * len(weights),)),
        ]
    if grads:
        scratch += [
            pltpu.VMEM((CHIPS, rows, D), bf16),
            pltpu.SemaphoreType.DMA((LANES * len(sizes),)),
        ]
    made = pl.pallas_call(
        kernel,
        out_shape=list(outs) + grad_shapes + list(far_out),
        grid=(1,),
        in_specs=[pl.BlockSpec(memory_space=pltpu.SMEM)]
        + [whole_block(x) for x in ins]
        + [hbm] * (n_buf + len(far_in)),
        out_specs=[whole_block(x) for x in outs] + [hbm] * (n_grad + len(far_out)),
        scratch_shapes=scratch,
        compiler_params=pltpu.CompilerParams(vmem_limit_bytes=(60 if far_in else 46) * 1024 * 1024),
        cost_estimate=pl.CostEstimate(
            flops=int(micros * MICRO), bytes_accessed=0, transcendentals=0
        ),
        name=name,
    )(meta, *ins, *hbm_in, *far_in)
    return made[:n_out], made[n_out:]


PARAMS = (
    "b_query",
    "b_value",
    "b_out",
    "gain_one",
    "bias_one",
    "b_image",
    "cb_query",
    "cb_value",
    "cb_out",
    "gain_two",
    "bias_two",
    "b_outer",
    "gain_three",
    "bias_three",
)
B_INNER = 16


def param(ref, name):
    at = PARAMS.index(name)
    return ref[at : at + 1]


def join_params(*vectors):
    def kernel(*refs):
        out = refs[-1]
        for i, ref in enumerate(refs[:-2]):
            out[i : i + 1] = ref[...].reshape(1, D)
        out[len(PARAMS) : B_INNER] = jnp.zeros((B_INNER - len(PARAMS), D), f32)
        inner = refs[-2][...].reshape(1, FF)
        for k in range(4):
            out[B_INNER + k : B_INNER + k + 1] = inner[:, k * D : (k + 1) * D]
        out[B_INNER + 4 :] = jnp.zeros((4, D), f32)

    vmem = pl.BlockSpec(memory_space=pltpu.VMEM)
    return pl.pallas_call(
        kernel,
        out_shape=shape(24, D, dtype=f32),
        in_specs=[vmem] * len(vectors),
        out_specs=vmem,
        name="join_params",
    )(*vectors)


def pack_shards(core, shards):
    rows = sum(s.shape[0] * (s.shape[1] // D) for s in shards)

    def kernel(core_ref, *refs):
        parts = []
        for ref in refs[:-2]:
            full = ref[...].astype(f32)
            parts += [full[:, k * D : (k + 1) * D] for k in range(full.shape[1] // D)]
        full = jnp.concatenate(parts, axis=0)
        second = core_ref[0] > 0
        low, high = full[:, :HALF], full[:, HALF:]
        refs[-2][...] = jnp.where(second, high, low).astype(bf16)
        refs[-1][...] = jnp.where(second, low, high).astype(bf16)

    vmem = pl.BlockSpec(memory_space=pltpu.VMEM)
    return pl.pallas_call(
        kernel,
        out_shape=[shape(rows, HALF)] * 2,
        in_specs=[pl.BlockSpec(memory_space=pltpu.SMEM)] + [vmem] * len(shards),
        out_specs=[vmem] * 2,
        name="pack_shards",
    )(core[None].astype(jnp.int32), *shards)


def small_call(kernel, name, core, ins, outs):
    vmem = pl.BlockSpec(memory_space=pltpu.VMEM)
    return pl.pallas_call(
        kernel,
        out_shape=outs,
        in_specs=[pl.BlockSpec(memory_space=pltpu.SMEM)] + [vmem] * len(ins),
        out_specs=[vmem] * len(outs),
        name=name,
    )(core[None].astype(jnp.int32), *ins)


def split_cores(core, pieces):
    rows = sum(sum(sizes) for _, sizes in pieces) // 2

    def kernel(core_ref, *refs):
        second = core_ref[0] > 0
        out = 0
        for i, (_, sizes) in enumerate(pieces):
            total = refs[4 * i][...].astype(f32)
            for ref in refs[4 * i + 1 : 4 * i + 4]:
                total = total + ref[...].astype(f32)
            at = 0
            for size in sizes:
                half = size // 2
                low, high = total[at : at + half], total[at + half : at + size]
                refs[-2][out : out + half] = jnp.where(second, high, low)
                refs[-1][out : out + half] = jnp.where(second, low, high)
                at, out = at + size, out + half

    ins = [term for terms, _ in pieces for term in terms]
    return small_call(kernel, "split_cores", core, ins, [shape(rows, HALF, dtype=f32)] * 2)


def join_halves(core, mine, came, counts):
    def kernel(core_ref, mine_ref, came_ref, *outs):
        second, at = core_ref[0] > 0, 0
        for out, (rows, wide) in zip(outs, counts):
            for k in range(wide):
                a, b = mine_ref[at : at + rows], came_ref[at : at + rows]
                out[:, k * D : k * D + HALF] = jnp.where(second, b, a)
                out[:, k * D + HALF : (k + 1) * D] = jnp.where(second, a, b)
                at += rows

    outs = [shape(rows, wide * D, dtype=f32) for rows, wide in counts]
    return small_call(kernel, "join_halves", core, [mine, came], outs)


def shape(*dims, dtype=bf16):
    return jax.ShapeDtypeStruct(dims, dtype)


def first_front(meta, ready, weight, put, ins, outs):
    text, images, params = ins
    q, k, v, attn, image_rows, ck, cv = outs
    ready(0)
    rows = text[:TR]
    q[...] = (mm(rows, weight(0)) + param(params, "b_query")).astype(bf16)
    k[...] = mm(rows, weight(1)).astype(bf16)
    v[...] = (mm(rows, weight(2)) + param(params, "b_value")).astype(bf16)
    self_forward(q, k, v, attn, meta)
    ready(1)
    image_rows[...] = (mm(images[...], weight(3)) + param(params, "b_image")).astype(bf16)
    ck[...] = mm(image_rows[...], weight(4)).astype(bf16)
    cv[...] = (mm(image_rows[...], weight(5)) + param(params, "cb_value")).astype(bf16)


def mid_front(meta, ready, weight, put, ins, outs):
    text, attn, ck, cv, params = ins
    hidden, cq, cross, joint, sum_one, sum_two = outs
    ready(0)
    ready(1)
    sum_one[...] = text[:TR].astype(f32) + (mm(attn[...], weight(0)) + param(params, "b_out"))
    normed, _ = ln_parts(sum_one[...])
    hidden[...] = (normed * param(params, "gain_one") + param(params, "bias_one")).astype(bf16)
    cq[...] = (mm(hidden[...], weight(1)) + param(params, "cb_query")).astype(bf16)
    attend_forward(cq, ck, cv, cross, IP, lambda i: NP)
    sum_two[...] = hidden[...].astype(f32) + (mm(cross[...], weight(2)) + param(params, "cb_out"))
    normed, _ = ln_parts(sum_two[...])
    joint[...] = (normed * param(params, "gain_two") + param(params, "bias_two")).astype(bf16)


def feed_forward(meta, ready, weight, put, ins, outs):
    joint, cot, sum_two, params = ins
    mixed, grad_sum_two, vec_three, vec_two = outs[:4]
    outer_hbm, grad_outer_hbm, outer_w, grad_outer_w, active, slope, grad_inner, sem = outs[4:]
    load = pltpu.make_async_copy(outer_hbm, outer_w, sem.at[0])
    load.start()
    ready(0)
    ready(1)
    for k in range(4):
        lanes = slice(k * D, (k + 1) * D)
        pre = mm(joint[...], weight(k)) + params[B_INNER + k : B_INNER + k + 1]
        cdf = 0.5 * (1.0 + lax.erf(pre * 0.5**0.5))
        active[:, lanes] = (pre * cdf).astype(bf16)
        slope[:, lanes] = cdf + pre * (jnp.exp(-0.5 * pre * pre) * 0.3989422804014327)
    load.wait()
    outer = mm(active[...], outer_w[...]) + param(params, "b_outer")
    normed, scale = ln_parts(joint[...].astype(f32) + outer)
    gain = param(params, "gain_three")
    result = normed * gain + param(params, "bias_three")
    row = lax.broadcasted_iota(jnp.int32, (TP, 1), 0)
    keep = [jnp.where(row < meta[2 + i], 1.0, 0.0) for i in range(ITEMS)]
    for i in range(ITEMS):
        mixed[i] = (result[i * TP : (i + 1) * TP] * keep[i])[:SEQ]
    grad = cot[...].astype(f32) * jnp.concatenate(keep, axis=0)
    grad_sum = ln_back(grad, normed, scale, gain)
    grad_outer = grad_sum.astype(bf16)
    vec_three[0:1] = rowsum(grad * normed)
    vec_three[1:2] = rowsum(grad)
    vec_three[2:3] = rowsum(grad_outer)
    vec_three[3:4] = jnp.zeros((1, D), f32)
    grad_outer_w[...] = mm_w(active[...], grad_outer).astype(bf16)
    store = pltpu.make_async_copy(grad_outer_w, grad_outer_hbm, sem.at[1])
    store.start()
    for k in range(4):
        lanes = slice(k * D, (k + 1) * D)
        part = (slope[:, lanes] * mm_t(grad_outer, outer_w[lanes, :])).astype(bf16)
        grad_inner[:, lanes] = part
        vec_three[4 + k : 5 + k] = rowsum(part)
        put(k, mm_w(joint[...], part))
    grad = grad_sum
    for k in range(4):
        grad = grad + mm_t(grad_inner[:, k * D : (k + 1) * D], weight(k))
    normed, scale = ln_parts(sum_two[...])
    grad_sum_two[...] = ln_back(grad, normed, scale, param(params, "gain_two"))
    vec_two[...] = jnp.concatenate(
        [rowsum(grad * normed), rowsum(grad), jnp.zeros((6, D), f32)], axis=0
    )
    store.wait()


def mid_back(meta, ready, weight, put, ins, outs):
    grad_sum_two, cross, hidden, attn, cq, ck, cv, sum_one, params = ins
    grad_sum_one, grad_attn, dk, dv, vec, dq, grad_cross = outs
    gain = param(params, "gain_one")
    grad_cross_branch = grad_sum_two[...].astype(bf16)
    ready(0)
    ready(1)
    grad_cross[...] = mm_t(grad_cross_branch, weight(2)).astype(bf16)
    attend_backward(grad_cross, cq, ck, cv, dq, dk, dv, IP, lambda i: NP)
    put(2, mm_w(cross[...], grad_cross_branch))
    put(1, mm_w(hidden[...], dq[...]))
    grad = grad_sum_two[...] + mm_t(dq[...], weight(1))
    normed, scale = ln_parts(sum_one[...])
    grad_sum_one[...] = ln_back(grad, normed, scale, gain)
    grad_branch = grad_sum_one[...].astype(bf16)
    put(0, mm_w(attn[...], grad_branch))
    grad_attn[...] = mm_t(grad_branch, weight(0)).astype(bf16)
    vec[...] = jnp.concatenate(
        [
            rowsum(grad_cross_branch),
            rowsum(dq[...]),
            rowsum(grad * normed),
            rowsum(grad),
            rowsum(grad_branch),
            jnp.zeros((3, D), f32),
        ],
        axis=0,
    )


def image_back(meta, ready, weight, put, ins, outs):
    images, image_rows, dk, dv = ins
    grad_patches, vec = outs
    put(1, mm_w(image_rows[...], dk[...]))
    put(2, mm_w(image_rows[...], dv[...]))
    ready(0)
    grad_image = (mm_t(dk[...], weight(1)) + mm_t(dv[...], weight(2))).astype(bf16)
    put(0, mm_w(images[...], grad_image))
    for i in range(ITEMS):
        grad_patches[i] = mm_t(grad_image[i * IP : (i + 1) * IP], weight(0))[:NP]
    vec[...] = jnp.concatenate([rowsum(dv[...]), rowsum(grad_image), jnp.zeros((6, D), f32)], axis=0)


def self_back(meta, ready, weight, put, ins, outs):
    grad_attn, q, k, v, text, grad_sum_one = ins
    grad_text, vec, dq, dk, dv = outs
    self_backward(grad_attn, q, k, v, dq, dk, dv, meta)
    put(0, mm_w(text[:TR], dq[...]))
    put(1, mm_w(text[:TR], dk[...]))
    put(2, mm_w(text[:TR], dv[...]))
    ready(0)
    total = grad_sum_one[...] + mm_t(dq[...], weight(0))
    total = total + mm_t(dk[...], weight(1))
    grad_text[...] = (total + mm_t(dv[...], weight(2))).astype(bf16)
    vec[...] = jnp.concatenate([rowsum(dq[...]), rowsum(dv[...]), jnp.zeros((6, D), f32)], axis=0)


def local(
    text,
    lengths,
    patches,
    w_query,
    w_key,
    w_value,
    w_out,
    b_query,
    b_value,
    b_out,
    gain_one,
    bias_one,
    w_image,
    b_image,
    c_query,
    c_key,
    c_value,
    c_out,
    cb_query,
    cb_value,
    cb_out,
    gain_two,
    bias_two,
    w_inner,
    b_inner,
    w_outer,
    b_outer,
    gain_three,
    bias_three,
    cotangent,
):
    count = lax.axis_size("mod") * lax.axis_size("dp")
    fold = count // LANES
    device = lax.axis_index("mod") * lax.axis_size("dp") + lax.axis_index("dp")
    place = device // fold
    core, chip = place % 2, place // 2
    first_core = core == 0

    def flip_device(block, mask):
        return lax.ppermute(block, AXES, [(i, i ^ mask) for i in range(count)])

    def flip_chip(block, mask):
        return flip_device(block, mask * 2 * fold)

    def flip_core(block):
        return flip_device(block, fold)

    def swap(block):
        return lax.ppermute(block, "mod", [(0, 1), (1, 0)])

    def gather_fold(shard):
        step = 1
        while step < fold:
            other = flip_device(shard, step)
            low = (device // step) % 2 == 0
            shard = jnp.concatenate(
                [jnp.where(low, shard, other), jnp.where(low, other, shard)], axis=0
            )
            step *= 2
        return shard

    def scatter_fold(total):
        step = fold // 2
        while step >= 1:
            low = (device // step) % 2 == 0
            half = total.shape[0] // 2
            kept = jnp.where(low, total[:half], total[half:])
            total = kept + flip_device(jnp.where(low, total[half:], total[:half]), step)
            step //= 2
        return total

    def split_rows(blocks, sizes):
        at, parts = 0, []
        for size in sizes:
            parts.append(blocks[..., at : at + size, :])
            at += size
        return parts

    def own_blocks(groups):
        kept, sent = pack_shards(core, [gather_fold(s) for g in groups for s in g])
        came = flip_core(sent)
        lows, highs = jnp.where(first_core, kept, came), jnp.where(first_core, came, kept)
        blocks, at = [], 0
        for g in groups:
            parts = []
            for shard in g:
                for _ in range(shard.shape[1] // D):
                    count = shard.shape[0] * fold
                    parts += [lows[at : at + count], highs[at : at + count]]
                    at += count
            blocks.append(jnp.concatenate(parts, axis=0))
        return blocks

    def spread(blocks, masks):
        return [flip_chip(blocks, m) for m in masks]

    def reduce_core(bufs):
        return [bufs[0], flip_core(bufs[1])]

    def add(*terms):
        return sum(t.astype(f32) for t in terms)

    def reduce_last(groups, terms):
        at, far = 0, []
        for pack, count in groups:
            out = add(*[t[8:, at : at + count] for t in terms]).astype(bf16)
            far.append(flip_chip(out, PACKS[pack][2][0]))
            at += count
        return far

    def parts_of(groups, terms, far):
        at, parts = 0, []
        for (pack, count), came in zip(groups, far):

            def total(low, high, at=at, count=count, came=came):
                return add(*[t[low:high, at : at + count] for t in terms], came[low:high])

            parts.append((pack, total))
            at += count
        return parts

    def reduce_across(parts):
        blocks = []
        for pack in ("a", "b"):
            totals = [total for name, total in parts if name == pack]
            sent = jnp.concatenate([t(4, 8).astype(bf16) for t in totals], axis=1)
            blocks.append(flip_chip(sent, PACKS[pack][1][0]))
        return blocks

    def four_blocks(parts, across):
        blocks = []
        for pack, came in zip(("a", "b"), across):
            kept = jnp.concatenate([total(0, 4) for name, total in parts if name == pack], axis=1)
            blocks.append(add(kept, came).astype(bf16))
        return jnp.concatenate(blocks, axis=1)

    def reduce_z(blocks):
        return [blocks[0]] + [flip_chip(blocks[j], ZS[j]) for j in range(1, 4)]

    def finish(pieces, counts):
        mine, theirs = split_cores(core, pieces)
        return [scatter_fold(w) for w in join_halves(core, mine, flip_core(theirs), counts)]

    def sum_near(total):
        step = 1
        while step <= fold:
            total = total + flip_device(total, step)
            step *= 2
        return total

    def hold(values, *after):
        count = len(values)
        return list(lax.optimization_barrier(tuple(values) + after)[:count])

    text_rows = jnp.pad(text, ((0, 0), (0, TP - SEQ), (0, 0))).reshape(TR, D)
    lengths_row = jnp.pad(lengths.astype(bf16)[None], ((0, 15), (0, D - ITEMS)))
    text_rows = swap(jnp.concatenate([text_rows, lengths_row], axis=0))
    item_lengths = text_rows[TR, :ITEMS]
    cot_rows = jnp.pad(cotangent, ((0, 0), (0, TP - SEQ), (0, 0))).reshape(TR, D)
    meta = jnp.concatenate([chip[None], core[None], item_lengths.astype(jnp.int32)]).astype(jnp.int32)
    images = jnp.pad(patches, ((0, 0), (0, IP - NP), (0, 0))).reshape(IR, VW)
    params = join_params(
        *(b_query, b_value, b_out, gain_one, bias_one, b_image, cb_query),
        *(cb_value, cb_out, gain_two, bias_two, b_outer, gain_three, bias_three, b_inner),
    )
    w_outer = lax.all_gather(w_outer, AXES, axis=0, tiled=True)
    first, middle = own_blocks(
        [[w_query, w_key, w_value, c_query, c_out, w_image, c_key, c_value, w_out], [w_inner]]
    )
    first = jnp.stack([first] + spread(first, ZS[1:]))
    ma = jnp.stack([middle[:96], flip_chip(middle[:96], X)])
    mb = jnp.stack([middle[96:], flip_chip(middle[96:], Y)])
    middle = jnp.concatenate([ma, mb], axis=1)
    middle = jnp.concatenate([middle, flip_chip(middle, Z0)])
    a_4, b_4, ma, mb = hold(
        [first[:, :240], first[:, 240:], middle[:, :96], middle[:, 96:]], text_rows
    )
    a_8 = jnp.concatenate([a_4, flip_chip(a_4, X)])
    b_8 = jnp.concatenate([b_4, flip_chip(b_4, Y)])
    ma = jnp.concatenate([ma, flip_chip(ma, Z1)])
    a_8, b_8, ma, mb = hold([a_8, b_8, ma, mb])
    mb = jnp.concatenate([mb, flip_chip(mb, Z1)])
    a_far, b_far = flip_chip(a_8, Y), flip_chip(b_8, X)
    a_side, b_side = flip_core(a_8), flip_core(b_8)
    ma, mb, a_far, b_far, cot_rows = hold([ma, mb, a_far, b_far, cot_rows], a_side, b_side)
    cot_rows = swap(cot_rows)
    pack_a = [a_8, a_far, a_side, flip_core(a_far)]
    pack_b = [b_8, b_far, b_side, flip_core(b_far)]
    ma_far, mb_far = flip_chip(ma, Y), flip_chip(mb, X)
    qkv, img = ("a", pack_a, 0, 144), ("b", pack_b, 0, 160)
    mid = [("b", pack_b, 160, 48), ("a", pack_a, 144, 96)]
    qkv_sizes, img_sizes, mid_sizes = (48,) * 3, (64, 48, 48), (48,) * 3
    inner_sizes = (48,) * 4

    text_shape, image_shape = shape(TR, D), shape(IR, D)
    wide = shape(TR, D, dtype=f32)
    vec_shape = shape(8, D, dtype=f32)
    (q, k, v, attn, image_rows, ck, cv), _ = piece_kernel(
        first_front,
        "first_front",
        10,
        meta,
        [qkv, img],
        qkv_sizes + img_sizes,
        [],
        [text_rows, images, params],
        [text_shape] * 4 + [image_shape] * 3,
    )
    ma, mb, ma_far, mb_far, image_rows = hold([ma, mb, ma_far, mb_far, image_rows])
    inner = [
        ("ia", [ma, ma_far, flip_core(ma), flip_core(ma_far)], 0, 96),
        ("ib", [mb, mb_far, flip_core(mb), flip_core(mb_far)], 0, 96),
    ]
    (hidden, cq, cross, joint, sum_one, sum_two), _ = piece_kernel(
        mid_front,
        "mid_front",
        6,
        meta,
        mid,
        mid_sizes,
        [],
        [text_rows, attn, ck, cv, params],
        [text_shape] * 4 + [wide] * 2,
    )
    inner_groups, mid_groups = [("a", 96), ("b", 96)], [("b", 96), ("a", 48)]
    img_groups, qkv_groups = [("b", 160)], [("a", 144)]
    (mixed, grad_sum_two, vec_outer, vec_inner), (*inner_bufs, grad_w_outer) = piece_kernel(
        feed_forward,
        "feed_forward",
        17,
        meta,
        inner,
        inner_sizes,
        inner_groups,
        [joint, cot_rows, sum_two, params],
        [shape(ITEMS, SEQ, D, dtype=f32), wide, vec_shape, vec_shape],
        (
            [w_outer],
            [shape(FF, D)],
            [pltpu.VMEM((FF, D), bf16)] * 2
            + [pltpu.VMEM((TR, FF), bf16), pltpu.VMEM((TR, FF), f32), pltpu.VMEM((TR, FF), bf16)]
            + [pltpu.SemaphoreType.DMA((2,))],
        ),
    )
    grad_w_outer = lax.psum_scatter(grad_w_outer, AXES, scatter_dimension=0, tiled=True)
    inner_terms = reduce_core(inner_bufs)
    (grad_sum_one, grad_attn, dk, dv, vec_mid), mid_bufs = piece_kernel(
        mid_back,
        "mid_back",
        14,
        meta,
        mid,
        mid_sizes,
        mid_groups,
        [grad_sum_two, cross, hidden, attn, cq, ck, cv, sum_one, params],
        [wide, text_shape, image_shape, image_shape, vec_shape],
        ((), (), [pltpu.VMEM((TR, D), bf16)] * 2),
    )
    dk, mixed_out, *inner_terms = hold([dk, swap(mixed), *inner_terms])
    inner_far = reduce_last(inner_groups, inner_terms)
    mid_terms = reduce_core(mid_bufs)
    (grad_patches, vec_image), img_bufs = piece_kernel(
        image_back,
        "image_back",
        12,
        meta,
        [img],
        img_sizes,
        img_groups,
        [images, image_rows, dk, dv],
        [shape(ITEMS, NP, VW, dtype=f32), vec_shape],
    )
    img_terms = reduce_core(img_bufs)
    grad_attn, *held = hold([grad_attn, vec_image, *mid_terms, *inner_far])
    vec_image, mid_terms, inner_far = held[0], held[1:3], held[3:]
    mid_far = reduce_last(mid_groups, mid_terms)
    inner_parts = parts_of(inner_groups, inner_terms, inner_far)
    inner_across = reduce_across(inner_parts)
    (grad_text, vec_self), qkv_bufs = piece_kernel(
        self_back,
        "self_back",
        13,
        meta,
        [qkv],
        qkv_sizes,
        qkv_groups,
        [grad_attn, q, k, v, text_rows, grad_sum_one],
        [text_shape, vec_shape],
        ((), (), [pltpu.VMEM((TR, D), bf16)] * 3),
    )
    grad_patches, *held = hold(
        [grad_patches, vec_self, *qkv_bufs, *img_terms, *mid_far, *inner_across]
    )
    vec_self, qkv_bufs, img_terms = held[0], held[1:3], held[3:5]
    mid_far, inner_across = held[5:7], held[7:]
    qkv_terms = reduce_core(qkv_bufs)
    both_far = reduce_last(img_groups, img_terms) + reduce_last(qkv_groups, qkv_terms)
    rows = [vec_outer[:3], vec_outer[4:8], vec_inner[:2], vec_mid[:5], vec_image[:2], vec_self[:2]]
    vecs = sum_near(jnp.concatenate(rows + [jnp.zeros((6, D), f32)], axis=0))
    vecs = sum([flip_chip(vecs, z) for z in ZS[1:]], vecs)
    inner_blocks = four_blocks(inner_parts, inner_across)
    inner_blocks, vecs, *both_far = hold([inner_blocks, vecs, *both_far])
    parts = (
        parts_of(mid_groups, mid_terms, mid_far)
        + parts_of(img_groups, img_terms, both_far[:1])
        + parts_of(qkv_groups, qkv_terms, both_far[1:])
    )
    across = reduce_across(parts)
    inner_terms = reduce_z(inner_blocks)
    vecs, grad_text, *held = hold([vecs, grad_text, *across, *inner_terms])
    across, inner_terms = held[:2], held[2:]
    terms = reduce_z(four_blocks(parts, across))
    vecs = sum([flip_chip(vecs, m) for m in (X, Y, X | Y)], vecs)
    grad_text = swap(grad_text).reshape(ITEMS, TP, D)[:, :SEQ].astype(f32)
    vecs, *inner_terms = hold([vecs, *inner_terms])
    (grad_w_inner,) = finish([(inner_terms, inner_sizes)], [(24, 4)])
    (
        grad_c_out,
        grad_w_query,
        grad_w_key,
        grad_w_value,
        grad_w_out,
        grad_c_query,
        grad_w_image,
        grad_c_key,
        grad_c_value,
    ) = finish([(terms, (48,) * 6 + img_sizes)], [(24, 1)] * 6 + [(32, 1)] + [(24, 1)] * 2)
    return (
        mixed_out,
        grad_text,
        grad_patches,
        grad_w_query,
        grad_w_key,
        grad_w_value,
        grad_w_out,
        vecs[16],
        vecs[17],
        vecs[13],
        vecs[11],
        vecs[12],
        grad_w_image,
        vecs[15],
        grad_c_query,
        grad_c_key,
        grad_c_value,
        grad_c_out,
        vecs[10],
        vecs[14],
        vecs[9],
        vecs[7],
        vecs[8],
        grad_w_inner,
        vecs[3:7].reshape(FF),
        grad_w_outer.astype(f32),
        vecs[2],
        vecs[0],
        vecs[1],
    )


def solution(mesh):
    items = P(AXES, None, None)
    shard, whole = P(AXES, None), P()
    in_specs = (
        (items, P(AXES), items)
        + (shard,) * 4
        + (whole,) * 5
        + (shard, whole)
        + (shard,) * 4
        + (whole,) * 5
        + (shard, whole, shard)
        + (whole,) * 3
        + (items,)
    )
    out_specs = (
        (items,) * 3
        + (shard,) * 4
        + (whole,) * 5
        + (shard, whole)
        + (shard,) * 4
        + (whole,) * 5
        + (shard, whole, shard)
        + (whole,) * 3
    )
    return jax.shard_map(local, mesh=mesh, in_specs=in_specs, out_specs=out_specs, check_vma=False)
```
